128 devices in a mesh: section: 8 (over z_lo, x), peer: 16 (over z_hi, y, core).
Axes of the slice: x: 4, y: 4, z: 4 (z_hi: 2, z_lo: 2; z = z_hi * 2 + z_lo), core: 2. Of those that a mesh axis runs over, the one named last changes fastest.
Arguments:
- acts: bfloat16 [8, 16, 384, 2560], P('section', 'peer'), may hold values from -6 to 6
- saved: bfloat16 [8, 16, 384, 2560], P('section', 'peer'), may hold values from -6 to 6
- cotangent: bfloat16 [8, 16, 384, 2560], P('section', 'peer'), may hold values from -6 to 6
- weight: bfloat16 [8, 2560, 2560], P('section', 'peer'), may hold values from -0.125 to 0.125
- gain: float32 [8, 2560], P('section'), may hold values from 0.1 to 1.9
- route: int32 [8, 16, 16, 1], P('section', 'peer'), may hold values from 0 to 15; in each aligned block of 16 rows (0 to 15, 16 to 31, ..., all dimensions but the last counted through in order) at most 2 rows name the same one
Outputs:
- next_acts: bfloat16 [8, 16, 768, 2560], P('section', 'peer')
- next_grads: bfloat16 [8, 16, 768, 2560], P('section', 'peer')
- weight_grad: float32 [8, 2560, 2560], P('section', 'peer')
The draws below stay inside these ranges and needn't reach their ends.
Inputs may be any that keep to these rules, and one draw needn't show every extreme that they name: route[s, p, b, 0] is the peer that block b of peer p's forward arrival at section s is delivered to, and the peer of section s - 1 (the sections in a loop) that block b of its input gradient returns to. No peer is named more than 2 times among the 16 blocks of one peer, and in every draw some peer is named exactly 2 times.
All inputs are finite; a program needn't handle non-finite values.
Results may differ from the reference program's by a relative error of at most 0.015.
Values may be sent and summed in bfloat16 or wider, within the bound.
A program may use at most 128 MiB of HBM per device.

```python
import math
from functools import partial
import jax
import jax.numpy as jnp
import numpy as np
from jax import lax

D = 2560
TOK = 384
BLOCKS = 16
MOST = 2
SECTIONS = 8
PEERS = 16
N_PEER = 16


def block_scale(own_key, shape, split, least, largest):
    level = 1.0
    for axis_at, parts in split:
        heights = jax.random.uniform(jax.random.fold_in(jax.random.fold_in(own_key, 6), axis_at), (parts,), jnp.float32, least / len(split), largest / len(split))
        level = level * jnp.repeat(jnp.exp(heights), shape[axis_at] // parts).reshape((-1,) + (1,) * (len(shape) - 1 - axis_at))
    return level


def shared_out(key, own, number, rows, number_of, top, most, skew):
    sequence = jax.random.permutation(key, number_of)
    packed, ordinary = portions_of(number_of, rows * top, most, skew, True), portions_of(number_of, rows * top, most, skew, False)
    places = jnp.arange(number_of)

    def named(lengths, rotation):
        used = int((lengths > 0).sum())
        fixed = max(1, used // 4)
        shifted = fixed + (places - fixed + rotation * (used - fixed)) % max(1, number_of - fixed)
        return jnp.zeros((number_of,), jnp.int32).at[sequence[jnp.where(places < fixed, places, shifted)]].set(jnp.asarray(lengths, jnp.int32))

    lengths = jnp.where(number % 4 == 0, named(packed, number // 4), named(ordinary, number - number // 4 - 1))
    mixed = jax.random.permutation(jax.random.fold_in(own, 3), number_of)
    donor, taker = mixed[0:number_of // 2 * 2:2], mixed[1:number_of // 2 * 2:2]
    room = jnp.minimum(lengths[donor] - 1, most - lengths[taker]) // 2
    room = jnp.where((donor == sequence[0]) | (taker == sequence[0]) | (lengths[taker] == 0), 0, jnp.maximum(room, 0))
    shifted = jax.random.randint(jax.random.fold_in(own, 4), (number_of // 2,), 0, 1 << 20) % (room + 1)
    lengths = lengths.at[donor].add(-shifted).at[taker].add(shifted)
    members = jnp.searchsorted(jnp.cumsum(lengths), jnp.arange(rows * top), side="right").astype(jnp.int32)
    table = members.reshape(top, rows).T
    table = table[jax.random.permutation(jax.random.fold_in(own, 1), rows)]
    rotation = jax.random.randint(jax.random.fold_in(own, 2), (rows, 1), 0, top)
    return jnp.take_along_axis(table, (jnp.arange(top)[None, :] + rotation) % top, axis=1)


def portions_of(number_of, total, bound, lean, full):
    portions = [(1 << 20) // math.isqrt(rank ** lean) + 1 for rank in range(1, number_of + 1)]
    largest = bound if full else min(bound, max(-(-total // number_of), total * portions[0] // sum(portions)))
    least = 1 if total - largest >= number_of - 1 else 0
    counts, spare = [largest] + [least] * (number_of - 1), total - largest - least * (number_of - 1)
    while spare > 0:
        candidates = [i for i in range(1, number_of) if counts[i] < largest] or [i for i in range(1, number_of) if counts[i] < bound]
        mass, budget = sum([portions[i] for i in candidates]), spare
        for i in candidates:
            addition = min(bound - counts[i], max(1, budget * portions[i] // mass), spare)
            counts[i] = counts[i] + addition
            spare = spare - addition
    return np.array(counts)


def scatter_about(own_key, shape, deviation, most, shards=(), kind=jnp.bfloat16):
    array = deviation * jax.random.normal(own_key, shape, jnp.float32)
    if shards:
        array = array * block_scale(own_key, shape, shards, -0.22, 0.18)
    return jnp.clip(array, -most, most).astype(kind)


def setup_inputs(seed: int = 0) -> dict:
    splits = jax.random.split(jax.random.key(seed), 7)
    acts = scatter_about(splits[0], (SECTIONS, PEERS, TOK, D), 1.0, 6.0, ((0, 8), (1, 16)))
    saved = scatter_about(splits[1], (SECTIONS, PEERS, TOK, D), 1.0, 6.0, ((0, 8), (1, 16)))
    cotangent = scatter_about(splits[2], (SECTIONS, PEERS, TOK, D), 1.0, 6.0, ((0, 8), (1, 16)))
    weight = scatter_about(splits[3], (SECTIONS, D, D), D ** -0.5, 0.125, ((0, 8), (1, 16)))
    gain = jnp.clip(1.0 + 0.18 * jax.random.normal(splits[4], (SECTIONS, D), jnp.float32), 0.1, 1.9)
    route_keys = jax.random.split(jax.random.fold_in(splits[5], 1), SECTIONS * PEERS * BLOCKS // BLOCKS)
    route_turns = jax.random.permutation(jax.random.fold_in(splits[5], 3), SECTIONS * PEERS * BLOCKS // BLOCKS)
    route = jax.vmap(lambda own, number: shared_out(jax.random.fold_in(splits[5], 2), own, number, BLOCKS, N_PEER, 1, MOST, 2))(route_keys, route_turns).reshape((SECTIONS, PEERS, BLOCKS, 1))
    return {"acts": acts, "saved": saved, "cotangent": cotangent, "weight": weight, "gain": gain, "route": route}


EPS = 1e-05

def norm_rows(rows, gain_row):
    wide = rows.astype(jnp.float32)
    inverse = lax.rsqrt(lax.optimization_barrier(jnp.mean(wide * wide, axis=-1, keepdims=True)) + EPS)
    unit_rows = wide * inverse
    return ((unit_rows * gain_row).astype(jnp.bfloat16), unit_rows, inverse)

def silu_slope(values):
    sigma = jax.nn.sigmoid(values)
    return sigma * (1.0 + values * (1.0 - sigma))

def packing(route_row, peers, most):
    blocks_count = route_row.shape[0]
    row_order = lax.broadcasted_iota(jnp.int32, (blocks_count, blocks_count), 0)
    col_order = lax.broadcasted_iota(jnp.int32, (blocks_count, blocks_count), 1)
    matches = (route_row[:, None] == route_row[None, :]) & (col_order < row_order)
    ranking = lax.optimization_barrier(jnp.sum(matches.astype(jnp.int32), axis=1)).astype(jnp.int32)
    target = (route_row * most + ranking).astype(jnp.int32)
    slot_ids = lax.broadcasted_iota(jnp.int32, (peers * most, blocks_count), 0)
    return (slot_ids == target[None, :]).astype(jnp.bfloat16)

def section_pass(operands):
    fresh, stored, upstream, weight_section, gain_section = operands
    gain_row = gain_section.astype(jnp.float32)
    peers, tokens, width = fresh.shape
    fresh_rows = fresh.reshape(-1, width)
    normed_in = norm_rows(fresh_rows, gain_row)[0]
    pre_in = jnp.dot(normed_in, weight_section, preferred_element_type=jnp.float32)
    output_rows = (fresh_rows.astype(jnp.float32) + jax.nn.silu(pre_in)).astype(jnp.bfloat16)
    normed_saved, unit_saved, inv_saved = norm_rows(stored.reshape(-1, width), gain_row)
    pre_saved = jnp.dot(normed_saved, weight_section, preferred_element_type=jnp.float32)
    upstream_rows = upstream.reshape(-1, width).astype(jnp.float32)
    slope = (upstream_rows * silu_slope(pre_saved)).astype(jnp.bfloat16)
    back_norm = lax.dot_general(slope, weight_section, (((1,), (1,)), ((), ())), preferred_element_type=jnp.float32)
    scaled = back_norm * gain_row
    centre = lax.optimization_barrier(jnp.mean(scaled * unit_saved, axis=-1, keepdims=True))
    input_grad = (upstream_rows + inv_saved * (scaled - unit_saved * centre)).astype(jnp.bfloat16)

    def add_peer(total, pair):
        left, right = pair
        term = lax.dot_general(left, right, (((0,), (0,)), ((), ())), preferred_element_type=jnp.float32) / tokens
        term = lax.optimization_barrier(term.astype(jnp.bfloat16))
        return (total + term.astype(jnp.float32), None)
    weight_grad, unused = lax.scan(add_peer, jnp.zeros((width, width), jnp.float32), (normed_saved.reshape(peers, tokens, width), slope.reshape(peers, tokens, width)))
    return (output_rows.reshape(peers, tokens, width), input_grad.reshape(peers, tokens, width), weight_grad)

def deliver(operands):
    table, rows = operands
    peers, tokens, width = rows.shape
    blocks_count = table.shape[2]
    most = table.shape[1] // peers
    flat = rows.reshape(peers, blocks_count, -1).astype(jnp.float32)
    sent = jnp.einsum('pkb,pbe->pke', table.astype(jnp.float32), flat)
    sent = sent.reshape(peers, peers, most * (tokens // blocks_count), width)
    return jnp.transpose(sent, (1, 0, 2, 3)).reshape(peers, -1, width).astype(jnp.bfloat16)

def reference(acts, saved, cotangent, weight, gain, route):
    output_rows, input_grad, weight_grad = lax.map(section_pass, (acts, saved, cotangent, weight, gain))
    make_table = partial(packing, peers=PEERS, most=MOST)
    tables = jax.vmap(jax.vmap(make_table))(route[..., 0])
    next_acts = lax.map(deliver, (tables, jnp.roll(output_rows, 1, axis=0)))
    next_grads = jnp.roll(lax.map(deliver, (tables, input_grad)), -1, axis=0)
    return (next_acts, next_grads, weight_grad)
```

```python
import functools

import jax
import jax.numpy as jnp
from jax import lax
from jax.experimental import pallas as pl
from jax.experimental.pallas import tpu as pltpu
from jax.sharding import PartitionSpec as P

MESH = pl.DeviceIdType.MESH
F32 = jnp.float32
BF16 = jnp.bfloat16
MOST = 2
EPS = 1e-05

A = 96

ORDER = (
    (1, 2, 0), (1, 2, 1), (0, 2, 0), (1, 1, 0), (0, 3, 1), (1, 3, 0), (0, 1, 1), (1, 1, 1),
    (0, 3, 0), (1, 3, 1), (0, 1, 0), (0, 2, 1), (1, 0, 0), (1, 0, 1), (0, 0, 1),
)
SLOTS = 96


def kernel(
    acts, saved, cot, w, gain, route,
    next_acts, next_grads, wgrad,
    full, acts_v, saved_v, cot_v, chunks, acc, turned, turned_out, slopes, inverse,
    terms, half_a, side_a, far_a, far_b, half_b, side_b, rows_f, rows_b, perm, targets, targets_next,
    send_sem, recv_sem, local_sem,
):
    shard, width = w.shape
    tokens = acts.shape[0]
    chip = 2 * shard
    sections = lax.axis_size("section")
    s = lax.axis_index("section")
    p = lax.axis_index("peer")
    zh, y, c = p // 8, lax.rem(p // 2, 4), lax.rem(p, 2)
    zo, co = 1 - zh, 1 - c
    yp, ym, y2 = lax.rem(y + 1, 4), lax.rem(y + 3, 4), lax.rem(y + 2, 4)
    sp, sm = lax.rem(s + 1, sections), lax.rem(s + sections - 1, sections)

    def peer(zz, yy, cc):
        return (s, zz * 8 + yy * 2 + cc)

    right, left, across, core = peer(zh, yp, c), peer(zh, ym, c), peer(zo, y, c), peer(zh, y, co)

    tags = {}
    sent = []

    def slot(tag):
        return tags.setdefault(tag, len(tags))

    def send(tag, src, dst, device):
        copy = pltpu.make_async_remote_copy(
            src_ref=src, dst_ref=dst, send_sem=send_sem.at[slot(tag)],
            recv_sem=recv_sem.at[slot(tag)], device_id=device, device_id_type=MESH,
        )
        copy.start()
        sent.append(copy)
        return copy

    def arrive(tag, dst):
        pltpu.make_async_remote_copy(
            src_ref=dst, dst_ref=dst, send_sem=send_sem.at[slot(tag)],
            recv_sem=recv_sem.at[slot(tag)], device_id=core, device_id_type=MESH,
        ).wait_recv()

    loads = [
        pltpu.make_async_copy(src, dst, local_sem.at[i])
        for i, (src, dst) in enumerate(((saved, saved_v), (acts, acts_v), (cot, cot_v)))
    ]
    base = pl.multiple_of(p * shard, 32)
    own_rows = pltpu.make_async_copy(w, full.at[pl.ds(base, shard)], local_sem.at[3])
    own_rows.start()
    for copy in loads:
        copy.start()

    barrier = pltpu.get_barrier_semaphore()
    friends = [peer(zh ^ dz, lax.rem(y + dy, 4), c ^ dc) for dz, dy, dc in ORDER] + [(sp, p), (sm, p)]
    for device in friends:
        pl.semaphore_signal(barrier, inc=1, device_id=device, device_id_type=MESH)
    pl.semaphore_wait(barrier, len(friends))

    def region(zz, yy, cc, lo, hi):
        start = pl.multiple_of((zz * 8 + yy * 2 + cc) * shard + lo, 16)
        return full.at[pl.ds(start, hi - lo)]

    H, M = A // 2, A + (shard - A) // 2
    pieces = {
        "own": (zh, y, 0, shard),
        "zA": (zo, y, 0, A), "yA+": (zh, ym, 0, A), "yA-": (zh, yp, 0, A),
        "yB+": (zh, ym, A, shard), "yB-": (zh, yp, A, shard), "zB": (zo, y, A, shard),
        "A0": (zh, y2, 0, H), "A1": (zh, y2, H, A), "B0": (zh, y2, A, M), "B1": (zh, y2, M, shard),
        "wA+": (zo, ym, 0, A), "wA-": (zo, yp, 0, A), "wA0": (zo, y2, 0, H), "wA1": (zo, y2, H, A),
        "zB+": (zo, ym, A, shard), "zB-": (zo, yp, A, shard),
        "zB0": (zo, y2, A, M), "zB1": (zo, y2, M, shard),
    }

    def give(tag, lo, hi, device):
        send(tag, w.at[pl.ds(lo, hi - lo)], region(zh, y, c, lo, hi), device)

    give("yA+", 0, A, right)
    give("zA", 0, A, across)
    give("yA-", 0, A, left)
    give("yB+", A, shard, right)
    give("zB", A, shard, across)
    give("yB-", A, shard, left)
    give("c:own", 0, shard, core)

    def pass_on(tag, *onward):
        zz, yy, lo, hi = pieces[tag]
        arrive(tag, region(zz, yy, c, lo, hi))
        for new, device in onward:
            _, _, nlo, nhi = pieces[new] if new in ("A0", "A1", "B0", "B1", "wA0", "wA1") else pieces[tag]
            part = region(zz, yy, c, nlo, nhi)
            send(new, part, part, device)
        part = region(zz, yy, c, lo, hi)
        send("c:" + tag, part, part, core)

    def from_core(*names):
        for tag in names:
            zz, yy, lo, hi = pieces[tag]
            arrive("c:" + tag, region(zz, yy, co, lo, hi))

    named = [route[b] for b in range(route.shape[0])]
    block = tokens // len(named)
    lane = lax.broadcasted_iota(jnp.int32, targets.shape, 1)
    spot = jnp.zeros(targets.shape, jnp.int32)
    for b, r in enumerate(named):
        rank = jnp.int32(0)
        for other in named[:b]:
            rank = rank + jnp.where(other == r, 1, 0).astype(jnp.int32)
        first = (r * MOST + rank) * block - b * block
        spot = jnp.where((lane >= b * block) & (lane < (b + 1) * block), lane + first, spot)
    targets[...] = spot
    send("targets", targets, targets_next, (sm, p))

    gain_row = gain[...]
    step_rows = 32

    def normalise(source, offset, keep):
        def body(i, carry):
            at = pl.ds(pl.multiple_of(i * step_rows, step_rows), step_rows)
            wide = source[at, :].astype(F32)
            inv = lax.rsqrt(jnp.mean(wide * wide, axis=-1, keepdims=True) + EPS)
            normed = (wide * inv * gain_row).astype(BF16)
            to = pl.ds(pl.multiple_of(offset + i * step_rows, step_rows), step_rows)
            for k in range(width // chip):
                chunks[k, to, :] = normed[:, k * chip:(k + 1) * chip]
            if keep:
                inverse[at, :] = jnp.broadcast_to(inv, (step_rows, inverse.shape[1]))
            return carry

        lax.fori_loop(0, tokens // step_rows, body, 0)

    loads[0].wait()
    normalise(saved_v, 0, True)
    loads[1].wait()
    normalise(acts_v, tokens, False)

    columns = 512

    def multiply(zz, yy, start=False):
        k = zz * 4 + yy
        at = pl.ds(pl.multiple_of(k * chip, 64), chip)

        def body(i, carry):
            cols = pl.ds(pl.multiple_of(i * columns, columns), columns)
            part = jnp.dot(chunks[k], full[at, cols], preferred_element_type=F32)
            acc[:, cols] = part if start else acc[:, cols] + part
            return carry

        lax.fori_loop(0, width // columns, body, 0)

    own_rows.wait()
    from_core("own")
    multiply(zh, y, True)

    pass_on("zA", ("wA+", right), ("wA-", left))
    pass_on("yA+", ("A0", right))
    pass_on("yA-", ("A1", left))

    def turn(k, carry):
        flat = jnp.transpose(chunks[k, 0:tokens, :].astype(F32)).astype(BF16)
        low, high = flat[:shard], flat[shard:]
        to = pl.ds(pl.multiple_of((lax.rem(k, 4) * 2 + k // 4) * shard, 32), shard)
        turned[to, 0:tokens] = jnp.where(c == 0, low, high)
        turned_out[to, :] = jnp.where(c == 0, high, low)
        return carry

    lax.fori_loop(0, width // chip, turn, 0)
    send("turned", turned_out, turned.at[:, pl.ds(tokens, tokens)], core)

    pass_on("yB+", ("B0", right), ("zB+", across))
    pass_on("yB-", ("B1", left), ("zB-", across))
    pass_on("zB")
    from_core("yA+", "yB+")
    multiply(zh, ym)
    pass_on("A0")
    pass_on("A1")
    from_core("yA-", "yB-")
    multiply(zh, yp)
    pass_on("B0", ("zB0", across))
    pass_on("B1", ("zB1", across))
    from_core("zA", "zB")
    multiply(zo, y)
    pass_on("wA+", ("wA0", right))
    pass_on("wA-", ("wA1", left))
    from_core("A0", "A1", "B0", "B1")
    multiply(zh, y2)
    pass_on("zB+")
    pass_on("zB-")
    from_core("wA+", "zB+")
    multiply(zo, ym)
    pass_on("zB0")
    pass_on("zB1")
    from_core("wA-", "zB-")
    multiply(zo, yp)
    pass_on("wA0")
    pass_on("wA1")
    from_core("wA0", "wA1", "zB0", "zB1")
    multiply(zo, y2)

    loads[2].wait()
    gathered = list(sent)
    sent.clear()

    def slope_body(i, carry):
        at = pl.ds(pl.multiple_of(i * step_rows, step_rows), step_rows)
        v = acc[at, :]
        sigma = jax.nn.sigmoid(v)
        slopes[at, :] = (cot_v[at, :].astype(F32) * (sigma * (1.0 + v * (1.0 - sigma)))).astype(BF16)
        return carry

    lax.fori_loop(0, tokens // step_rows, slope_body, 0)
    send("slope", slopes.at[pl.ds(0, tokens)], slopes.at[pl.ds(tokens, tokens)], core)

    def output_body(i, carry):
        at = pl.ds(pl.multiple_of(i * step_rows, step_rows), step_rows)
        v = acc[pl.ds(pl.multiple_of(tokens + i * step_rows, step_rows), step_rows), :]
        acts_v[at, :] = (acts_v[at, :].astype(F32) + v * jax.nn.sigmoid(v)).astype(BF16)
        return carry

    lax.fori_loop(0, tokens // step_rows, output_body, 0)
    send("forward", acts_v, rows_f, (sp, p))

    arrive("turned", turned.at[:, pl.ds(tokens, tokens)])
    arrive("slope", slopes.at[pl.ds(tokens, tokens)])

    def term(k, yy):
        at = pl.ds(pl.multiple_of(yy * chip, 64), chip)

        def body(i, carry):
            cols = pl.ds(pl.multiple_of(i * columns, columns), columns)
            part = jnp.dot(turned[at, :], slopes[:, cols], preferred_element_type=F32) / tokens
            part = part.astype(BF16)
            terms[k, 0, :, cols] = part[:shard]
            terms[k, 1, :, cols] = part[shard:]
            return carry

        lax.fori_loop(0, width // columns, body, 0)

    def cross(k):
        send("tB%d" % k, terms.at[k, zo, pl.ds(A, shard - A)], far_b.at[k], across)

    lower, upper = pl.ds(0, H), pl.ds(H, H)
    last, last_low, last_high = pl.ds(A, shard - A), pl.ds(A, M - A), pl.ds(M, shard - M)
    term(0, y2)
    send("tA0", terms.at[0, :, lower], half_a.at[0], right)
    send("tA1", terms.at[0, :, upper], half_a.at[1], left)
    cross(0)
    term(1, yp)
    cross(1)
    term(2, ym)
    cross(2)
    term(3, y)
    cross(3)

    tile = 256

    def back_body(i, carry):
        at = pl.ds(pl.multiple_of(i * tile, tile), tile)
        acc[0:tokens, at] = lax.dot_general(
            slopes[0:tokens, :], full[at, :], (((1,), (1,)), ((), ())), preferred_element_type=F32
        )
        return carry

    lax.fori_loop(0, width // tile, back_body, 0)

    def add(target, lo, count, extra):
        size = 16

        def body(i, carry):
            at = pl.ds(pl.multiple_of(lo + i * size, size), size)
            here = pl.ds(pl.multiple_of(i * size, size), size)
            target[at, :] = (target[at, :].astype(F32) + extra[here, :].astype(F32)).astype(BF16)
            return carry

        lax.fori_loop(0, count // size, body, 0)

    arrive("tB0", far_b.at[0])
    add(terms.at[0, zh], A, shard - A, far_b.at[0])
    send("tb0", terms.at[0, zh, last_low], half_b.at[0], right)
    send("tb1", terms.at[0, zh, last_high], half_b.at[1], left)
    arrive("tA0", half_a.at[0])
    for z in range(2):
        add(terms.at[1, z], 0, H, half_a.at[0, z])
    send("tA+", terms.at[1, :, pl.ds(0, A)], side_a.at[0], right)
    arrive("tA1", half_a.at[1])
    for z in range(2):
        add(terms.at[2, z], H, H, half_a.at[1, z])
    send("tA-", terms.at[2, :, pl.ds(0, A)], side_a.at[1], left)

    def grad_body(i, carry):
        at = pl.ds(pl.multiple_of(i * step_rows, step_rows), step_rows)
        scaled = acc[at, :] * gain_row
        inv = inverse[at, 0:1]
        unit = saved_v[at, :].astype(F32) * inv
        centre = jnp.mean(scaled * unit, axis=-1, keepdims=True)
        cot_v[at, :] = (cot_v[at, :].astype(F32) + inv * (scaled - unit * centre)).astype(BF16)
        return carry

    lax.fori_loop(0, tokens // step_rows, grad_body, 0)
    send("backward", cot_v, rows_b, (sm, p))

    for k, tag, lo, count, device in ((1, "tb0", A, M - A, right), (2, "tb1", M, shard - M, left)):
        arrive("tB%d" % k, far_b.at[k])
        add(terms.at[k, zh], A, shard - A, far_b.at[k])
        arrive(tag, half_b.at[k - 1])
        add(terms.at[k, zh], lo, count, half_b.at[k - 1])
        send("tB" + "?+-"[k], terms.at[k, zh, last], side_b.at[k - 1], device)

    def pack(rows, where, at_row):
        size = 96

        def build(i, carry):
            at = pl.ds(pl.multiple_of(i * size, size), size)
            row = lax.broadcasted_iota(jnp.int32, (size, tokens), 0) + i * size
            perm[at, :] = jnp.where(row == where[0:1, :], 1.0, 0.0).astype(BF16)
            return carry

        lax.fori_loop(0, perm.shape[0] // size, build, 0)

        def body(i, carry):
            cols = pl.ds(pl.multiple_of(i * columns, columns), columns)
            full[at_row:at_row + perm.shape[0], cols] = jnp.dot(
                perm[...], rows[:, cols], preferred_element_type=F32
            ).astype(BF16)
            return carry

        lax.fori_loop(0, width // columns, body, 0)

    share = MOST * block

    def place(ref, number, offset=0):
        return ref.at[pl.ds(pl.multiple_of(offset + number * share, 16), share)]

    def scatter(name, out, offset, sem):
        local = pltpu.make_async_copy(place(full, p, offset), place(out, p), local_sem.at[sem])
        for i, (dz, dy, dc) in enumerate(ORDER):
            to = peer(zh ^ dz, lax.rem(y + dy, 4), c ^ dc)
            send("%s%d" % (name, i), place(full, to[1], offset), place(out, p), to)
        local.start()
        return local

    def collect(name, out):
        for i, (dz, dy, dc) in enumerate(ORDER):
            origin = peer(zh ^ dz, lax.rem(y + 4 - dy, 4), c ^ dc)
            arrive("%s%d" % (name, i), place(out, origin[1]))

    for copy in gathered:
        copy.wait_send()

    arrive("tA+", side_a.at[0])
    arrive("tA-", side_a.at[1])
    for z in range(2):
        add(terms.at[3, z], 0, A, side_a.at[0, z])
        add(terms.at[3, z], 0, A, side_a.at[1, z])
    send("tzA", terms.at[3, zo, pl.ds(0, A)], far_a, across)

    arrive("forward", rows_f)
    pack(rows_f, targets, 0)
    local_f = scatter("f", next_acts, 0, 4)
    arrive("targets", targets_next)
    arrive("backward", rows_b)
    pack(rows_b, targets_next, perm.shape[0])
    local_b = scatter("b", next_grads, perm.shape[0], 5)

    arrive("tzA", far_a)
    arrive("tB3", far_b.at[3])
    arrive("tB+", side_b.at[0])
    arrive("tB-", side_b.at[1])
    size = 16

    def last_a(i, carry):
        at = pl.ds(pl.multiple_of(i * size, size), size)
        to = pl.ds(pl.multiple_of(tokens + i * size, size), size)
        acc[to, :] = terms[3, zh, at, :].astype(F32) + far_a[at, :].astype(F32)
        return carry

    lax.fori_loop(0, A // size, last_a, 0)

    def last_b(i, carry):
        here = pl.ds(pl.multiple_of(i * size, size), size)
        at = pl.ds(pl.multiple_of(A + i * size, size), size)
        to = pl.ds(pl.multiple_of(tokens + A + i * size, size), size)
        acc[to, :] = (
            (terms[3, zh, at, :].astype(F32) + far_b[3, here, :].astype(F32))
            + (side_b[0, here, :].astype(F32) + side_b[1, here, :].astype(F32))
        )
        return carry

    lax.fori_loop(0, (shard - A) // size, last_b, 0)
    store = pltpu.make_async_copy(acc.at[pl.ds(tokens, shard)], wgrad, local_sem.at[6])
    store.start()

    collect("f", next_acts)
    collect("b", next_grads)
    store.wait()
    local_f.wait()
    local_b.wait()
    for copy in sent:
        copy.wait_send()
    assert len(tags) <= SLOTS, len(tags)


def local(acts, saved, cotangent, weight, gain, route):
    tokens, width = acts.shape[2:]
    shard = weight.shape[1]
    peers = width // shard
    packed = MOST * tokens
    hbm = pl.BlockSpec(memory_space=pl.ANY)
    v = pltpu.VMEM
    next_acts, next_grads, weight_grad = pl.pallas_call(
        kernel,
        out_shape=(
            jax.ShapeDtypeStruct((packed, width), BF16),
            jax.ShapeDtypeStruct((packed, width), BF16),
            jax.ShapeDtypeStruct((shard, width), F32),
        ),
        in_specs=[hbm] * 4 + [pl.BlockSpec(memory_space=v), pl.BlockSpec(memory_space=pltpu.SMEM)],
        out_specs=(hbm, hbm, hbm),
        scratch_shapes=[
            v((width, width), BF16),
            v((tokens, width), BF16), v((tokens, width), BF16), v((tokens, width), BF16),
            v((peers // 2, 2 * tokens, 2 * shard), BF16),
            v((2 * tokens, width), F32),
            v((width // 2, 2 * tokens), BF16), v((width // 2, tokens), BF16),
            v((2 * tokens, width), BF16),
            v((tokens, 128), F32),
            v((4, 2, shard, width), BF16),
            v((2, 2, A // 2, width), BF16),
            v((2, 2, A, width), BF16),
            v((A, width), BF16),
            v((4, shard - A, width), BF16),
            v((2, (shard - A) // 2, width), BF16),
            v((2, shard - A, width), BF16),
            v((tokens, width), BF16), v((tokens, width), BF16),
            v((packed, tokens), BF16),
            v((8, tokens), jnp.int32), v((8, tokens), jnp.int32),
            pltpu.SemaphoreType.DMA((SLOTS,)),
            pltpu.SemaphoreType.DMA((SLOTS,)),
            pltpu.SemaphoreType.DMA((8,)),
        ],
        compiler_params=pltpu.CompilerParams(
            collective_id=0, has_side_effects=True, vmem_limit_bytes=62 << 20
        ),
        name="tick",
    )(acts[0, 0], saved[0, 0], cotangent[0, 0], weight[0], gain, route[0, 0, :, 0])
    return (next_acts[None, None], next_grads[None, None], weight_grad[None])


def solution(mesh):
    placed = (
        P("section", "peer", None, None),
        P("section", "peer", None, None),
        P("section", "peer", None, None),
        P("section", "peer", None),
        P("section", None),
        P("section", "peer", None, None),
    )
    return jax.shard_map(
        local,
        mesh=mesh,
        in_specs=placed,
        out_specs=(
            P("section", "peer", None, None),
            P("section", "peer", None, None),
            P("section", "peer", None),
        ),
        check_vma=False,
    )
```

```python
import functools

import jax
import jax.numpy as jnp
from jax import lax
from jax.experimental import pallas as pl
from jax.experimental.pallas import tpu as pltpu
from jax.sharding import PartitionSpec as P

MESH = pl.DeviceIdType.MESH
F32 = jnp.float32
BF16 = jnp.bfloat16
MOST = 2
EPS = 1e-05

A = 96

ORDER = (
    (1, 2, 0), (1, 2, 1), (0, 2, 0), (1, 1, 0), (0, 3, 1), (1, 3, 0), (0, 1, 1), (1, 1, 1),
    (0, 3, 0), (1, 3, 1), (0, 1, 0), (0, 2, 1), (1, 0, 0), (1, 0, 1), (0, 0, 1),
)
SLOTS = 96


def kernel(
    acts, saved, cot, w, gain, route,
    next_acts, next_grads, wgrad,
    full, acts_v, saved_v, cot_v, chunks, acc, turned, turned_out, slopes, inverse,
    terms, half_a, side_a, far_a, far_b, half_b, side_b, rows_f, rows_b, perm, targets, targets_next, targets_flip,
    send_sem, recv_sem, local_sem,
):
    shard, width = w.shape
    tokens = acts.shape[0]
    chip = 2 * shard
    s = lax.axis_index("section")
    p = lax.axis_index("peer")
    zh, y, c = p // 8, lax.rem(p // 2, 4), lax.rem(p, 2)
    zo, co = 1 - zh, 1 - c
    yp, ym, y2 = lax.rem(y + 1, 4), lax.rem(y + 3, 4), lax.rem(y + 2, 4)
    x, low = lax.rem(s, 4), (s // 4) * 4
    xp, xm, flipped = low + lax.rem(x + 1, 4), low + lax.rem(x + 3, 4), 4 - low + x

    def peer(zz, yy, cc):
        return (s, zz * 8 + yy * 2 + cc)

    right, left, across, core = peer(zh, yp, c), peer(zh, ym, c), peer(zo, y, c), peer(zh, y, co)

    tags = {}
    sent = {}

    def slot(tag):
        return tags.setdefault(tag, len(tags))

    def send(tag, src, dst, device):
        copy = pltpu.make_async_remote_copy(
            src_ref=src, dst_ref=dst, send_sem=send_sem.at[slot(tag)],
            recv_sem=recv_sem.at[slot(tag)], device_id=device, device_id_type=MESH,
        )
        copy.start()
        sent[tag] = copy

    def finished(*names):
        for tag in names:
            copy = sent.pop(tag)
            copy.wait_send()

    def arrive(tag, dst):
        pltpu.make_async_remote_copy(
            src_ref=dst, dst_ref=dst, send_sem=send_sem.at[slot(tag)],
            recv_sem=recv_sem.at[slot(tag)], device_id=core, device_id_type=MESH,
        ).wait_recv()

    loads = [
        pltpu.make_async_copy(src, dst, local_sem.at[i])
        for i, (src, dst) in enumerate(((saved, saved_v), (acts, acts_v), (cot, cot_v)))
    ]
    base = pl.multiple_of(p * shard, 32)
    own_rows = pltpu.make_async_copy(w, full.at[pl.ds(base, shard)], local_sem.at[3])
    own_rows.start()
    for copy in loads:
        copy.start()

    barrier = pltpu.get_barrier_semaphore()
    friends = [peer(zh ^ dz, lax.rem(y + dy, 4), c ^ dc) for dz, dy, dc in ORDER] + [(xp, p), (xm, p)]
    friends += [(flipped, i) for i in range(16)]
    for device in friends:
        pl.semaphore_signal(barrier, inc=1, device_id=device, device_id_type=MESH)
    pl.semaphore_wait(barrier, len(friends))

    def region(zz, yy, cc, lo, hi):
        start = pl.multiple_of((zz * 8 + yy * 2 + cc) * shard + lo, 16)
        return full.at[pl.ds(start, hi - lo)]

    H, M = A // 2, A + (shard - A) // 2
    pieces = {
        "own": (zh, y, 0, shard),
        "zA": (zo, y, 0, A), "yA+": (zh, ym, 0, A), "yA-": (zh, yp, 0, A),
        "yB+": (zh, ym, A, shard), "yB-": (zh, yp, A, shard), "zB": (zo, y, A, shard),
        "A0": (zh, y2, 0, H), "A1": (zh, y2, H, A), "B0": (zh, y2, A, M), "B1": (zh, y2, M, shard),
        "wA+": (zo, ym, 0, A), "wA-": (zo, yp, 0, A), "wA0": (zo, y2, 0, H), "wA1": (zo, y2, H, A),
        "zB+": (zo, ym, A, shard), "zB-": (zo, yp, A, shard),
        "zB0": (zo, y2, A, M), "zB1": (zo, y2, M, shard),
    }

    def give(tag, lo, hi, device):
        send(tag, w.at[pl.ds(lo, hi - lo)], region(zh, y, c, lo, hi), device)

    give("yA+", 0, A, right)
    give("zA", 0, A, across)
    give("yA-", 0, A, left)
    give("yB+", A, shard, right)
    give("zB", A, shard, across)
    give("yB-", A, shard, left)
    give("c:own", 0, shard, core)

    def pass_on(tag, *onward):
        zz, yy, lo, hi = pieces[tag]
        arrive(tag, region(zz, yy, c, lo, hi))
        for new, device in onward:
            _, _, nlo, nhi = pieces[new] if new in ("A0", "A1", "B0", "B1", "wA0", "wA1") else pieces[tag]
            part = region(zz, yy, c, nlo, nhi)
            send(new, part, part, device)
        part = region(zz, yy, c, lo, hi)
        send("c:" + tag, part, part, core)

    def from_core(*names):
        for tag in names:
            zz, yy, lo, hi = pieces[tag]
            arrive("c:" + tag, region(zz, yy, co, lo, hi))

    named = [route[b] for b in range(route.shape[0])]
    block = tokens // len(named)
    lane = lax.broadcasted_iota(jnp.int32, targets.shape, 1)
    spot = jnp.zeros(targets.shape, jnp.int32)
    for b, r in enumerate(named):
        rank = jnp.int32(0)
        for other in named[:b]:
            rank = rank + jnp.where(other == r, 1, 0).astype(jnp.int32)
        first = (r * MOST + rank) * block - b * block
        spot = jnp.where((lane >= b * block) & (lane < (b + 1) * block), lane + first, spot)
    targets[...] = spot
    send("targets", targets, targets_next, (xm, p))
    send("flip", targets, targets_flip, (flipped, p))

    gain_row = gain[...]
    step_rows = 32

    def normalise(source, offset, keep):
        def body(i, carry):
            at = pl.ds(pl.multiple_of(i * step_rows, step_rows), step_rows)
            wide = source[at, :].astype(F32)
            inv = lax.rsqrt(jnp.mean(wide * wide, axis=-1, keepdims=True) + EPS)
            normed = (wide * inv * gain_row).astype(BF16)
            to = pl.ds(pl.multiple_of(offset + i * step_rows, step_rows), step_rows)
            for k in range(width // chip):
                chunks[k, to, :] = normed[:, k * chip:(k + 1) * chip]
            if keep:
                inverse[at, :] = jnp.broadcast_to(inv, (step_rows, inverse.shape[1]))
            return carry

        lax.fori_loop(0, tokens // step_rows, body, 0)

    loads[0].wait()
    normalise(saved_v, 0, True)
    loads[1].wait()
    normalise(acts_v, tokens, False)

    columns = 512

    def multiply(zz, yy, start=False):
        k = zz * 4 + yy
        at = pl.ds(pl.multiple_of(k * chip, 64), chip)

        def body(i, carry):
            cols = pl.ds(pl.multiple_of(i * columns, columns), columns)
            part = jnp.dot(chunks[k], full[at, cols], preferred_element_type=F32)
            acc[:, cols] = part if start else acc[:, cols] + part
            return carry

        lax.fori_loop(0, width // columns, body, 0)

    own_rows.wait()
    from_core("own")
    multiply(zh, y, True)

    pass_on("zA", ("wA+", right), ("wA-", left))
    pass_on("yA+", ("A0", right))
    pass_on("yA-", ("A1", left))

    def turn(k, carry):
        flat = jnp.transpose(chunks[k, 0:tokens, :].astype(F32)).astype(BF16)
        low, high = flat[:shard], flat[shard:]
        to = pl.ds(pl.multiple_of((lax.rem(k, 4) * 2 + k // 4) * shard, 32), shard)
        turned[to, 0:tokens] = jnp.where(c == 0, low, high)
        turned_out[to, :] = jnp.where(c == 0, high, low)
        return carry

    lax.fori_loop(0, width // chip, turn, 0)
    send("turned", turned_out, turned.at[:, pl.ds(tokens, tokens)], core)

    pass_on("yB+", ("B0", right), ("zB+", across))
    pass_on("yB-", ("B1", left), ("zB-", across))
    pass_on("zB")
    from_core("yA+", "yB+")
    multiply(zh, ym)
    pass_on("A0")
    pass_on("A1")
    from_core("yA-", "yB-")
    multiply(zh, yp)
    pass_on("B0", ("zB0", across))
    pass_on("B1", ("zB1", across))
    from_core("zA", "zB")
    multiply(zo, y)
    pass_on("wA+", ("wA0", right))
    pass_on("wA-", ("wA1", left))
    from_core("A0", "A1", "B0", "B1")
    multiply(zh, y2)
    pass_on("zB+")
    pass_on("zB-")
    from_core("wA+", "zB+")
    multiply(zo, ym)
    pass_on("zB0")
    pass_on("zB1")
    from_core("wA-", "zB-")
    multiply(zo, yp)
    pass_on("wA0")
    pass_on("wA1")
    from_core("wA0", "wA1", "zB0", "zB1")
    multiply(zo, y2)

    loads[2].wait()
    gathered = list(sent)

    def slope_body(i, carry):
        at = pl.ds(pl.multiple_of(i * step_rows, step_rows), step_rows)
        v = acc[at, :]
        sigma = jax.nn.sigmoid(v)
        slopes[at, :] = (cot_v[at, :].astype(F32) * (sigma * (1.0 + v * (1.0 - sigma)))).astype(BF16)
        return carry

    lax.fori_loop(0, tokens // step_rows, slope_body, 0)
    send("slope", slopes.at[pl.ds(0, tokens)], slopes.at[pl.ds(tokens, tokens)], core)

    def output_body(i, carry):
        at = pl.ds(pl.multiple_of(i * step_rows, step_rows), step_rows)
        v = acc[pl.ds(pl.multiple_of(tokens + i * step_rows, step_rows), step_rows), :]
        acts_v[at, :] = (acts_v[at, :].astype(F32) + v * jax.nn.sigmoid(v)).astype(BF16)
        return carry

    lax.fori_loop(0, tokens // step_rows, output_body, 0)
    send("forward", acts_v, rows_f, (xp, p))

    arrive("turned", turned.at[:, pl.ds(tokens, tokens)])
    arrive("slope", slopes.at[pl.ds(tokens, tokens)])

    def term(k, yy):
        at = pl.ds(pl.multiple_of(yy * chip, 64), chip)

        def body(i, carry):
            cols = pl.ds(pl.multiple_of(i * columns, columns), columns)
            part = jnp.dot(turned[at, :], slopes[:, cols], preferred_element_type=F32) / tokens
            part = part.astype(BF16)
            terms[k, 0, :, cols] = part[:shard]
            terms[k, 1, :, cols] = part[shard:]
            return carry

        lax.fori_loop(0, width // columns, body, 0)

    def cross(k):
        send("tB%d" % k, terms.at[k, zo, pl.ds(A, shard - A)], far_b.at[k], across)

    lower, upper = pl.ds(0, H), pl.ds(H, H)
    last, last_low, last_high = pl.ds(A, shard - A), pl.ds(A, M - A), pl.ds(M, shard - M)
    term(0, y2)
    send("tA0", terms.at[0, :, lower], half_a.at[0], right)
    send("tA1", terms.at[0, :, upper], half_a.at[1], left)
    cross(0)
    term(1, yp)
    cross(1)
    term(2, ym)
    cross(2)
    term(3, y)
    cross(3)

    tile = 256

    def back_body(i, carry):
        at = pl.ds(pl.multiple_of(i * tile, tile), tile)
        acc[0:tokens, at] = lax.dot_general(
            slopes[0:tokens, :], full[at, :], (((1,), (1,)), ((), ())), preferred_element_type=F32
        )
        return carry

    lax.fori_loop(0, width // tile, back_body, 0)

    def grad_body(i, carry):
        at = pl.ds(pl.multiple_of(i * step_rows, step_rows), step_rows)
        scaled = acc[at, :] * gain_row
        inv = inverse[at, 0:1]
        unit = saved_v[at, :].astype(F32) * inv
        centre = jnp.mean(scaled * unit, axis=-1, keepdims=True)
        cot_v[at, :] = (cot_v[at, :].astype(F32) + inv * (scaled - unit * centre)).astype(BF16)
        return carry

    lax.fori_loop(0, tokens // step_rows, grad_body, 0)
    send("backward", cot_v, rows_b, (xm, p))

    def add(target, lo, count, extra):
        size = 16

        def body(i, carry):
            at = pl.ds(pl.multiple_of(lo + i * size, size), size)
            here = pl.ds(pl.multiple_of(i * size, size), size)
            target[at, :] = (target[at, :].astype(F32) + extra[here, :].astype(F32)).astype(BF16)
            return carry

        lax.fori_loop(0, count // size, body, 0)

    arrive("tB0", far_b.at[0])
    add(terms.at[0, zh], A, shard - A, far_b.at[0])
    send("tb0", terms.at[0, zh, last_low], half_b.at[0], right)
    send("tb1", terms.at[0, zh, last_high], half_b.at[1], left)
    arrive("tA0", half_a.at[0])
    for z in range(2):
        add(terms.at[1, z], 0, H, half_a.at[0, z])
    send("tA+", terms.at[1, :, pl.ds(0, A)], side_a.at[0], right)
    arrive("tA1", half_a.at[1])
    for z in range(2):
        add(terms.at[2, z], H, H, half_a.at[1, z])
    send("tA-", terms.at[2, :, pl.ds(0, A)], side_a.at[1], left)

    for k, tag, lo, count, device in ((1, "tb0", A, M - A, right), (2, "tb1", M, shard - M, left)):
        arrive("tB%d" % k, far_b.at[k])
        add(terms.at[k, zh], A, shard - A, far_b.at[k])
        arrive(tag, half_b.at[k - 1])
        add(terms.at[k, zh], lo, count, half_b.at[k - 1])
        send("tB" + "?+-"[k], terms.at[k, zh, last], side_b.at[k - 1], device)

    def pack(rows, where, at_row):
        size = 96

        def build(i, carry):
            at = pl.ds(pl.multiple_of(i * size, size), size)
            row = lax.broadcasted_iota(jnp.int32, (size, tokens), 0) + i * size
            perm[at, :] = jnp.where(row == where, 1.0, 0.0).astype(BF16)
            return carry

        lax.fori_loop(0, perm.shape[0] // size, build, 0)

        def body(i, carry):
            cols = pl.ds(pl.multiple_of(i * columns, columns), columns)
            full[at_row:at_row + perm.shape[0], cols] = jnp.dot(
                perm[...], rows[:, cols], preferred_element_type=F32
            ).astype(BF16)
            return carry

        lax.fori_loop(0, width // columns, body, 0)

    share = MOST * block

    def place(ref, number, offset=0):
        return ref.at[pl.ds(pl.multiple_of(offset + number * share, 16), share)]

    def scatter(name, out, offset, sem, flip):
        section = jnp.where(flip, flipped, s)
        for i, (dz, dy, dc) in enumerate(ORDER):
            to = peer(zh ^ dz, lax.rem(y + dy, 4), c ^ dc)[1]
            send("%s%d" % (name, i), place(full, to, offset), place(out, p), (section, to))
        away = pltpu.make_async_remote_copy(
            src_ref=place(full, p, offset), dst_ref=place(out, p), send_sem=send_sem.at[slot(name)],
            recv_sem=recv_sem.at[slot(name)], device_id=(flipped, p), device_id_type=MESH,
        )
        stay = pltpu.make_async_copy(place(full, p, offset), place(out, p), local_sem.at[sem])

        @pl.when(flip)
        def _():
            away.start()

        @pl.when(jnp.logical_not(flip))
        def _():
            stay.start()

        return away, stay, flip

    def collect(name, out, own):
        for i, (dz, dy, dc) in enumerate(ORDER):
            origin = peer(zh ^ dz, lax.rem(y + 4 - dy, 4), c ^ dc)[1]
            arrive("%s%d" % (name, i), place(out, origin))
        away, stay, flip = own

        @pl.when(flip)
        def _():
            away.wait()

        @pl.when(jnp.logical_not(flip))
        def _():
            stay.wait()

    finished(*gathered)

    arrive("tA+", side_a.at[0])
    arrive("tA-", side_a.at[1])
    for z in range(2):
        add(terms.at[3, z], 0, A, side_a.at[0, z])
        add(terms.at[3, z], 0, A, side_a.at[1, z])
    send("tzA", terms.at[3, zo, pl.ds(0, A)], far_a, across)

    arrive("flip", targets_flip)
    arrive("forward", rows_f)
    pack(rows_f, jnp.where(x == 0, targets_flip[0:1, :], targets[0:1, :]), 0)
    finished("backward")
    own_f = scatter("f", next_acts, 0, 4, x == 0)
    arrive("targets", targets_next)
    arrive("backward", rows_b)
    pack(rows_b, targets_next[0:1, :], perm.shape[0])
    finished(*["f%d" % i for i in range(len(ORDER))])
    own_b = scatter("b", next_grads, perm.shape[0], 5, x == 3)

    arrive("tzA", far_a)
    arrive("tB3", far_b.at[3])
    arrive("tB+", side_b.at[0])
    arrive("tB-", side_b.at[1])
    size = 16

    def last_a(i, carry):
        at = pl.ds(pl.multiple_of(i * size, size), size)
        to = pl.ds(pl.multiple_of(tokens + i * size, size), size)
        acc[to, :] = terms[3, zh, at, :].astype(F32) + far_a[at, :].astype(F32)
        return carry

    lax.fori_loop(0, A // size, last_a, 0)

    def last_b(i, carry):
        here = pl.ds(pl.multiple_of(i * size, size), size)
        at = pl.ds(pl.multiple_of(A + i * size, size), size)
        to = pl.ds(pl.multiple_of(tokens + A + i * size, size), size)
        acc[to, :] = (
            (terms[3, zh, at, :].astype(F32) + far_b[3, here, :].astype(F32))
            + (side_b[0, here, :].astype(F32) + side_b[1, here, :].astype(F32))
        )
        return carry

    lax.fori_loop(0, (shard - A) // size, last_b, 0)
    store = pltpu.make_async_copy(acc.at[pl.ds(tokens, shard)], wgrad, local_sem.at[6])
    store.start()

    collect("f", next_acts, own_f)
    collect("b", next_grads, own_b)
    store.wait()
    finished(*list(sent))
    assert len(tags) <= SLOTS, len(tags)


def local(acts, saved, cotangent, weight, gain, route):
    tokens, width = acts.shape[2:]
    shard = weight.shape[1]
    peers = width // shard
    packed = MOST * tokens
    hbm = pl.BlockSpec(memory_space=pl.ANY)
    v = pltpu.VMEM
    next_acts, next_grads, weight_grad = pl.pallas_call(
        kernel,
        out_shape=(
            jax.ShapeDtypeStruct((packed, width), BF16),
            jax.ShapeDtypeStruct((packed, width), BF16),
            jax.ShapeDtypeStruct((shard, width), F32),
        ),
        in_specs=[hbm] * 4 + [pl.BlockSpec(memory_space=v), pl.BlockSpec(memory_space=pltpu.SMEM)],
        out_specs=(hbm, hbm, hbm),
        scratch_shapes=[
            v((width, width), BF16),
            v((tokens, width), BF16), v((tokens, width), BF16), v((tokens, width), BF16),
            v((peers // 2, 2 * tokens, 2 * shard), BF16),
            v((2 * tokens, width), F32),
            v((width // 2, 2 * tokens), BF16), v((width // 2, tokens), BF16),
            v((2 * tokens, width), BF16),
            v((tokens, 128), F32),
            v((4, 2, shard, width), BF16),
            v((2, 2, A // 2, width), BF16),
            v((2, 2, A, width), BF16),
            v((A, width), BF16),
            v((4, shard - A, width), BF16),
            v((2, (shard - A) // 2, width), BF16),
            v((2, shard - A, width), BF16),
            v((tokens, width), BF16), v((tokens, width), BF16),
            v((packed, tokens), BF16),
            v((8, tokens), jnp.int32), v((8, tokens), jnp.int32), v((8, tokens), jnp.int32),
            pltpu.SemaphoreType.DMA((SLOTS,)),
            pltpu.SemaphoreType.DMA((SLOTS,)),
            pltpu.SemaphoreType.DMA((8,)),
        ],
        compiler_params=pltpu.CompilerParams(
            collective_id=0, has_side_effects=True, vmem_limit_bytes=62 << 20
        ),
        name="tick",
    )(acts[0, 0], saved[0, 0], cotangent[0, 0], weight[0], gain, route[0, 0, :, 0])
    return (next_acts[None, None], next_grads[None, None], weight_grad[None])


def solution(mesh):
    placed = (
        P("section", "peer", None, None),
        P("section", "peer", None, None),
        P("section", "peer", None, None),
        P("section", "peer", None),
        P("section", None),
        P("section", "peer", None, None),
    )
    return jax.shard_map(
        local,
        mesh=mesh,
        in_specs=placed,
        out_specs=(
            P("section", "peer", None, None),
            P("section", "peer", None, None),
            P("section", "peer", None),
        ),
        check_vma=False,
    )
```

```python
import functools

import jax
import jax.numpy as jnp
from jax import lax
from jax.experimental import pallas as pl
from jax.experimental.pallas import tpu as pltpu
from jax.sharding import PartitionSpec as P

MESH = pl.DeviceIdType.MESH
F32 = jnp.float32
BF16 = jnp.bfloat16
MOST = 2
EPS = 1e-05

A = 96

ORDER = (
    (1, 2, 0), (1, 2, 1), (0, 2, 0), (1, 1, 0), (0, 3, 1), (1, 3, 0), (0, 1, 1), (1, 1, 1),
    (0, 3, 0), (1, 3, 1), (0, 1, 0), (0, 2, 1), (1, 0, 0), (1, 0, 1), (0, 0, 1),
)
SLOTS = 96
STEPS = 4


def kernel(
    acts, saved, cot, w, gain, route,
    next_acts, next_grads, wgrad,
    full, acts_v, saved_v, cot_v, chunks, acc, turned, turned_out, slopes, inverse,
    terms, half_a, side_a, far_a, far_b, half_b, side_b, rows_f, rows_b, perm, targets, targets_next, targets_flip,
    send_sem, recv_sem, local_sem,
):
    shard, width = w.shape
    tokens = acts.shape[0]
    chip = 2 * shard
    s = lax.axis_index("section")
    p = lax.axis_index("peer")
    zh, y, c = p // 8, lax.rem(p // 2, 4), lax.rem(p, 2)
    zo, co = 1 - zh, 1 - c
    yp, ym, y2 = lax.rem(y + 1, 4), lax.rem(y + 3, 4), lax.rem(y + 2, 4)
    x, low = lax.rem(s, 4), (s // 4) * 4
    xp, xm, flipped = low + lax.rem(x + 1, 4), low + lax.rem(x + 3, 4), 4 - low + x

    def peer(zz, yy, cc):
        return (s, zz * 8 + yy * 2 + cc)

    right, left, across, core = peer(zh, yp, c), peer(zh, ym, c), peer(zo, y, c), peer(zh, y, co)

    tags = {}
    sent = {}

    def slot(tag):
        return tags.setdefault(tag, len(tags))

    def send(tag, src, dst, device):
        copy = pltpu.make_async_remote_copy(
            src_ref=src, dst_ref=dst, send_sem=send_sem.at[slot(tag)],
            recv_sem=recv_sem.at[slot(tag)], device_id=device, device_id_type=MESH,
        )
        copy.start()
        sent[tag] = copy

    def finished(*names):
        for tag in names:
            copy = sent.pop(tag)
            copy.wait_send()

    def arrive(tag, dst):
        pltpu.make_async_remote_copy(
            src_ref=dst, dst_ref=dst, send_sem=send_sem.at[slot(tag)],
            recv_sem=recv_sem.at[slot(tag)], device_id=core, device_id_type=MESH,
        ).wait_recv()

    loads = [
        pltpu.make_async_copy(src, dst, local_sem.at[i])
        for i, (src, dst) in enumerate(((saved, saved_v), (acts, acts_v), (cot, cot_v)))
    ]
    base = pl.multiple_of(p * shard, 32)
    own_rows = pltpu.make_async_copy(w, full.at[pl.ds(base, shard)], local_sem.at[3])
    own_rows.start()
    for copy in loads:
        copy.start()

    barrier = pltpu.get_barrier_semaphore()
    friends = [peer(zh ^ dz, lax.rem(y + dy, 4), c ^ dc) for dz, dy, dc in ORDER] + [(xp, p), (xm, p)]
    friends += [(flipped, i) for i in range(16)]
    for device in friends:
        pl.semaphore_signal(barrier, inc=1, device_id=device, device_id_type=MESH)
    pl.semaphore_wait(barrier, len(friends))

    def region(zz, yy, cc, lo, hi):
        start = pl.multiple_of((zz * 8 + yy * 2 + cc) * shard + lo, 16)
        return full.at[pl.ds(start, hi - lo)]

    H, M = A // 2, A + (shard - A) // 2
    pieces = {
        "own": (zh, y, 0, shard),
        "zA": (zo, y, 0, A), "yA+": (zh, ym, 0, A), "yA-": (zh, yp, 0, A),
        "yB+": (zh, ym, A, shard), "yB-": (zh, yp, A, shard), "zB": (zo, y, A, shard),
        "A0": (zh, y2, 0, H), "A1": (zh, y2, H, A), "B0": (zh, y2, A, M), "B1": (zh, y2, M, shard),
        "wA+": (zo, ym, 0, A), "wA-": (zo, yp, 0, A), "wA0": (zo, y2, 0, H), "wA1": (zo, y2, H, A),
        "zB+": (zo, ym, A, shard), "zB-": (zo, yp, A, shard),
        "zB0": (zo, y2, A, M), "zB1": (zo, y2, M, shard),
    }

    def give(tag, lo, hi, device):
        send(tag, w.at[pl.ds(lo, hi - lo)], region(zh, y, c, lo, hi), device)

    give("yA+", 0, A, right)
    give("zA", 0, A, across)
    give("yA-", 0, A, left)
    give("yB+", A, shard, right)
    give("zB", A, shard, across)
    give("yB-", A, shard, left)
    give("c:own", 0, shard, core)

    def pass_on(tag, *onward):
        zz, yy, lo, hi = pieces[tag]
        arrive(tag, region(zz, yy, c, lo, hi))
        for new, device in onward:
            _, _, nlo, nhi = pieces[new] if new in ("A0", "A1", "B0", "B1", "wA0", "wA1") else pieces[tag]
            part = region(zz, yy, c, nlo, nhi)
            send(new, part, part, device)
        part = region(zz, yy, c, lo, hi)
        send("c:" + tag, part, part, core)

    def from_core(*names):
        for tag in names:
            zz, yy, lo, hi = pieces[tag]
            arrive("c:" + tag, region(zz, yy, co, lo, hi))

    named = [route[b] for b in range(route.shape[0])]
    block = tokens // len(named)
    lane = lax.broadcasted_iota(jnp.int32, targets.shape, 1)
    spot = jnp.zeros(targets.shape, jnp.int32)
    for b, r in enumerate(named):
        rank = jnp.int32(0)
        for other in named[:b]:
            rank = rank + jnp.where(other == r, 1, 0).astype(jnp.int32)
        first = (r * MOST + rank) * block - b * block
        spot = jnp.where((lane >= b * block) & (lane < (b + 1) * block), lane + first, spot)
    targets[...] = spot
    send("targets", targets, targets_next, (xm, p))
    send("flip", targets, targets_flip, (flipped, p))

    gain_row = gain[...]
    step_rows = 32

    def normalise(source, offset, keep):
        def body(i, carry):
            at = pl.ds(pl.multiple_of(i * step_rows, step_rows), step_rows)
            wide = source[at, :].astype(F32)
            inv = lax.rsqrt(jnp.mean(wide * wide, axis=-1, keepdims=True) + EPS)
            normed = (wide * inv * gain_row).astype(BF16)
            to = pl.ds(pl.multiple_of(offset + i * step_rows, step_rows), step_rows)
            for k in range(width // chip):
                chunks[k, to, :] = normed[:, k * chip:(k + 1) * chip]
            if keep:
                inverse[at, :] = jnp.broadcast_to(inv, (step_rows, inverse.shape[1]))
            return carry

        lax.fori_loop(0, tokens // step_rows, body, 0)

    loads[0].wait()
    normalise(saved_v, 0, True)
    loads[1].wait()
    normalise(acts_v, tokens, False)

    columns = 512

    def multiply(zz, yy, start=False, part_rows=slice(None)):
        k = zz * 4 + yy
        at = pl.ds(pl.multiple_of(k * chip, 64), chip)

        def body(i, carry):
            cols = pl.ds(pl.multiple_of(i * columns, columns), columns)
            part = jnp.dot(chunks[k, part_rows, :], full[at, cols], preferred_element_type=F32)
            acc[part_rows, cols] = part if start else acc[part_rows, cols] + part
            return carry

        lax.fori_loop(0, width // columns, body, 0)

    own_rows.wait()
    from_core("own")
    multiply(zh, y, True)

    pass_on("zA", ("wA+", right), ("wA-", left))
    pass_on("yA+", ("A0", right))
    pass_on("yA-", ("A1", left))

    def turn(k, carry):
        flat = jnp.transpose(chunks[k, 0:tokens, :].astype(F32)).astype(BF16)
        low, high = flat[:shard], flat[shard:]
        to = pl.ds(pl.multiple_of((lax.rem(k, 4) * 2 + k // 4) * shard, 32), shard)
        turned[to, 0:tokens] = jnp.where(c == 0, low, high)
        turned_out[to, :] = jnp.where(c == 0, high, low)
        return carry

    lax.fori_loop(0, width // chip, turn, 0)
    send("turned", turned_out, turned.at[:, pl.ds(tokens, tokens)], core)

    pass_on("yB+", ("B0", right), ("zB+", across))
    pass_on("yB-", ("B1", left), ("zB-", across))
    pass_on("zB")
    from_core("yA+", "yB+")
    multiply(zh, ym)
    pass_on("A0")
    pass_on("A1")
    from_core("yA-", "yB-")
    multiply(zh, yp)
    pass_on("B0", ("zB0", across))
    pass_on("B1", ("zB1", across))
    from_core("zA", "zB")
    multiply(zo, y)
    pass_on("wA+", ("wA0", right))
    pass_on("wA-", ("wA1", left))
    from_core("A0", "A1", "B0", "B1")
    multiply(zh, y2)
    pass_on("zB+")
    pass_on("zB-")
    from_core("wA+", "zB+")
    multiply(zo, ym)
    pass_on("zB0")
    pass_on("zB1")
    from_core("wA-", "zB-")
    multiply(zo, yp)
    pass_on("wA0")
    pass_on("wA1")
    from_core("wA0", "wA1", "zB0", "zB1")
    multiply(zo, y2, part_rows=slice(0, tokens))

    loads[2].wait()
    gathered = list(sent)

    def slope_body(i, carry):
        at = pl.ds(pl.multiple_of(i * step_rows, step_rows), step_rows)
        v = acc[at, :]
        sigma = jax.nn.sigmoid(v)
        slopes[at, :] = (cot_v[at, :].astype(F32) * (sigma * (1.0 + v * (1.0 - sigma)))).astype(BF16)
        return carry

    lax.fori_loop(0, tokens // step_rows, slope_body, 0)
    send("slope", slopes.at[pl.ds(0, tokens)], slopes.at[pl.ds(tokens, tokens)], core)

    multiply(zo, y2, part_rows=slice(tokens, None))

    def output_body(i, carry):
        at = pl.ds(pl.multiple_of(i * step_rows, step_rows), step_rows)
        v = acc[pl.ds(pl.multiple_of(tokens + i * step_rows, step_rows), step_rows), :]
        acts_v[at, :] = (acts_v[at, :].astype(F32) + v * jax.nn.sigmoid(v)).astype(BF16)
        return carry

    lax.fori_loop(0, tokens // step_rows, output_body, 0)
    send("forward", acts_v, rows_f, (xp, p))

    arrive("turned", turned.at[:, pl.ds(tokens, tokens)])
    arrive("slope", slopes.at[pl.ds(tokens, tokens)])

    def term(k, yy):
        at = pl.ds(pl.multiple_of(yy * chip, 64), chip)

        def body(i, carry):
            cols = pl.ds(pl.multiple_of(i * columns, columns), columns)
            part = jnp.dot(turned[at, :], slopes[:, cols], preferred_element_type=F32) / tokens
            part = part.astype(BF16)
            terms[k, 0, :, cols] = part[:shard]
            terms[k, 1, :, cols] = part[shard:]
            return carry

        lax.fori_loop(0, width // columns, body, 0)

    def cross(k):
        send("tB%d" % k, terms.at[k, zo, pl.ds(A, shard - A)], far_b.at[k], across)

    lower, upper = pl.ds(0, H), pl.ds(H, H)
    last, last_low, last_high = pl.ds(A, shard - A), pl.ds(A, M - A), pl.ds(M, shard - M)
    term(0, y2)
    send("tA0", terms.at[0, :, lower], half_a.at[0], right)
    send("tA1", terms.at[0, :, upper], half_a.at[1], left)
    cross(0)
    term(1, yp)
    cross(1)
    term(2, ym)
    cross(2)
    term(3, y)
    cross(3)

    tile = 256

    def back_body(i, carry):
        at = pl.ds(pl.multiple_of(i * tile, tile), tile)
        acc[0:tokens, at] = lax.dot_general(
            slopes[0:tokens, :], full[at, :], (((1,), (1,)), ((), ())), preferred_element_type=F32
        )
        return carry

    lax.fori_loop(0, width // tile, back_body, 0)

    def grad_body(i, carry):
        at = pl.ds(pl.multiple_of(i * step_rows, step_rows), step_rows)
        scaled = acc[at, :] * gain_row
        inv = inverse[at, 0:1]
        unit = saved_v[at, :].astype(F32) * inv
        centre = jnp.mean(scaled * unit, axis=-1, keepdims=True)
        cot_v[at, :] = (cot_v[at, :].astype(F32) + inv * (scaled - unit * centre)).astype(BF16)
        return carry

    lax.fori_loop(0, tokens // step_rows, grad_body, 0)
    send("backward", cot_v, rows_b, (xm, p))

    def add(target, lo, count, extra):
        size = 16

        def body(i, carry):
            at = pl.ds(pl.multiple_of(lo + i * size, size), size)
            here = pl.ds(pl.multiple_of(i * size, size), size)
            target[at, :] = (target[at, :].astype(F32) + extra[here, :].astype(F32)).astype(BF16)
            return carry

        lax.fori_loop(0, count // size, body, 0)

    arrive("tB0", far_b.at[0])
    add(terms.at[0, zh], A, shard - A, far_b.at[0])
    send("tb0", terms.at[0, zh, last_low], half_b.at[0], right)
    send("tb1", terms.at[0, zh, last_high], half_b.at[1], left)
    arrive("tA0", half_a.at[0])
    for z in range(2):
        add(terms.at[1, z], 0, H, half_a.at[0, z])
    send("tA+", terms.at[1, :, pl.ds(0, A)], side_a.at[0], right)
    arrive("tA1", half_a.at[1])
    for z in range(2):
        add(terms.at[2, z], H, H, half_a.at[1, z])
    send("tA-", terms.at[2, :, pl.ds(0, A)], side_a.at[1], left)

    for k, tag, lo, count, device in ((1, "tb0", A, M - A, right), (2, "tb1", M, shard - M, left)):
        arrive("tB%d" % k, far_b.at[k])
        add(terms.at[k, zh], A, shard - A, far_b.at[k])
        arrive(tag, half_b.at[k - 1])
        add(terms.at[k, zh], lo, count, half_b.at[k - 1])
        send("tB" + "?+-"[k], terms.at[k, zh, last], side_b.at[k - 1], device)

    def pack(rows, where, at_row):
        size = 96

        def build(i, carry):
            at = pl.ds(pl.multiple_of(i * size, size), size)
            row = lax.broadcasted_iota(jnp.int32, (size, tokens), 0) + i * size
            perm[at, :] = jnp.where(row == where, 1.0, 0.0).astype(BF16)
            return carry

        lax.fori_loop(0, perm.shape[0] // size, build, 0)

        def body(i, carry):
            cols = pl.ds(pl.multiple_of(i * columns, columns), columns)
            full[at_row:at_row + perm.shape[0], cols] = jnp.dot(
                perm[...], rows[:, cols], preferred_element_type=F32
            ).astype(BF16)
            return carry

        lax.fori_loop(0, width // columns, body, 0)

    share = MOST * block

    def place(ref, number, offset=0):
        return ref.at[pl.ds(pl.multiple_of(offset + number * share, 16), share)]

    def scatter(name, out, offset, sem, flip):
        section = jnp.where(flip, flipped, s)
        for i, (dz, dy, dc) in enumerate(ORDER):
            to = peer(zh ^ dz, lax.rem(y + dy, 4), c ^ dc)[1]
            send("%s%d" % (name, i), place(full, to, offset), place(out, p), (section, to))
        away = pltpu.make_async_remote_copy(
            src_ref=place(full, p, offset), dst_ref=place(out, p), send_sem=send_sem.at[slot(name)],
            recv_sem=recv_sem.at[slot(name)], device_id=(flipped, p), device_id_type=MESH,
        )
        stay = pltpu.make_async_copy(place(full, p, offset), place(out, p), local_sem.at[sem])

        @pl.when(flip)
        def _():
            away.start()

        @pl.when(jnp.logical_not(flip))
        def _():
            stay.start()

        return away, stay, flip

    def collect(name, out, own):
        for i, (dz, dy, dc) in enumerate(ORDER):
            origin = peer(zh ^ dz, lax.rem(y + 4 - dy, 4), c ^ dc)[1]
            arrive("%s%d" % (name, i), place(out, origin))
        away, stay, flip = own

        @pl.when(flip)
        def _():
            away.wait()

        @pl.when(jnp.logical_not(flip))
        def _():
            stay.wait()

    finished(*gathered)

    arrive("tA+", side_a.at[0])
    arrive("tA-", side_a.at[1])
    for z in range(2):
        add(terms.at[3, z], 0, A, side_a.at[0, z])
        add(terms.at[3, z], 0, A, side_a.at[1, z])
    send("tzA", terms.at[3, zo, pl.ds(0, A)], far_a, across)

    arrive("flip", targets_flip)
    arrive("forward", rows_f)
    pack(rows_f, jnp.where(x == 0, targets_flip[0:1, :], targets[0:1, :]), 0)
    finished("backward")
    own_f = scatter("f", next_acts, 0, 4, x == 0)
    arrive("targets", targets_next)
    arrive("backward", rows_b)
    pack(rows_b, targets_next[0:1, :], perm.shape[0])
    finished(*["f%d" % i for i in range(len(ORDER))])
    own_b = scatter("b", next_grads, perm.shape[0], 5, x == 3)

    arrive("tzA", far_a)
    arrive("tB3", far_b.at[3])
    arrive("tB+", side_b.at[0])
    arrive("tB-", side_b.at[1])
    size = 16

    def last_a(i, carry):
        at = pl.ds(pl.multiple_of(i * size, size), size)
        to = pl.ds(pl.multiple_of(tokens + i * size, size), size)
        acc[to, :] = terms[3, zh, at, :].astype(F32) + far_a[at, :].astype(F32)
        return carry

    lax.fori_loop(0, A // size, last_a, 0)

    def last_b(i, carry):
        here = pl.ds(pl.multiple_of(i * size, size), size)
        at = pl.ds(pl.multiple_of(A + i * size, size), size)
        to = pl.ds(pl.multiple_of(tokens + A + i * size, size), size)
        acc[to, :] = (
            (terms[3, zh, at, :].astype(F32) + far_b[3, here, :].astype(F32))
            + (side_b[0, here, :].astype(F32) + side_b[1, here, :].astype(F32))
        )
        return carry

    lax.fori_loop(0, (shard - A) // size, last_b, 0)
    store = pltpu.make_async_copy(acc.at[pl.ds(tokens, shard)], wgrad, local_sem.at[6])
    store.start()

    collect("f", next_acts, own_f)
    collect("b", next_grads, own_b)
    store.wait()
    finished(*list(sent))
    assert len(tags) <= SLOTS, len(tags)


def move(acts, grads, sums, next_acts, next_grads, wgrad):
    next_acts[...] = acts[...]
    next_grads[...] = grads[...]
    wgrad[...] = sums[...]


def local(acts, saved, cotangent, weight, gain, route):
    tokens, width = acts.shape[2:]
    shard = weight.shape[1]
    peers = width // shard
    packed = MOST * tokens
    hbm = pl.BlockSpec(memory_space=pl.ANY)
    v = pltpu.VMEM
    next_acts, next_grads, weight_grad = pl.pallas_call(
        kernel,
        out_shape=(
            jax.ShapeDtypeStruct((packed, width), BF16),
            jax.ShapeDtypeStruct((packed, width), BF16),
            jax.ShapeDtypeStruct((shard, width), F32),
        ),
        in_specs=[hbm] * 4 + [pl.BlockSpec(memory_space=v), pl.BlockSpec(memory_space=pltpu.SMEM)],
        out_specs=(hbm, hbm, hbm),
        scratch_shapes=[
            v((width, width), BF16),
            v((tokens, width), BF16), v((tokens, width), BF16), v((tokens, width), BF16),
            v((peers // 2, 2 * tokens, 2 * shard), BF16),
            v((2 * tokens, width), F32),
            v((width // 2, 2 * tokens), BF16), v((width // 2, tokens), BF16),
            v((2 * tokens, width), BF16),
            v((tokens, 128), F32),
            v((4, 2, shard, width), BF16),
            v((2, 2, A // 2, width), BF16),
            v((2, 2, A, width), BF16),
            v((A, width), BF16),
            v((4, shard - A, width), BF16),
            v((2, (shard - A) // 2, width), BF16),
            v((2, shard - A, width), BF16),
            v((tokens, width), BF16), v((tokens, width), BF16),
            v((packed, tokens), BF16),
            v((8, tokens), jnp.int32), v((8, tokens), jnp.int32), v((8, tokens), jnp.int32),
            pltpu.SemaphoreType.DMA((SLOTS,)),
            pltpu.SemaphoreType.DMA((SLOTS,)),
            pltpu.SemaphoreType.DMA((8,)),
        ],
        compiler_params=pltpu.CompilerParams(
            collective_id=0, has_side_effects=True, vmem_limit_bytes=62 << 20
        ),
        name="tick",
    )(acts[0, 0], saved[0, 0], cotangent[0, 0], weight[0], gain, route[0, 0, :, 0])
    moved = (next_acts, next_grads, weight_grad)
    specs = [pl.BlockSpec((v.shape[0] // STEPS, width), lambda i: (i, 0)) for v in moved]
    next_acts, next_grads, weight_grad = pl.pallas_call(
        move,
        out_shape=tuple(jax.ShapeDtypeStruct(v.shape, v.dtype) for v in moved),
        grid=(STEPS,),
        in_specs=specs,
        out_specs=tuple(specs),
        compiler_params=pltpu.CompilerParams(vmem_limit_bytes=62 << 20),
        name="move",
    )(*moved)
    return (next_acts[None, None], next_grads[None, None], weight_grad[None])


def solution(mesh):
    placed = (
        P("section", "peer", None, None),
        P("section", "peer", None, None),
        P("section", "peer", None, None),
        P("section", "peer", None),
        P("section", None),
        P("section", "peer", None, None),
    )
    return jax.shard_map(
        local,
        mesh=mesh,
        in_specs=placed,
        out_specs=(
            P("section", "peer", None, None),
            P("section", "peer", None, None),
            P("section", "peer", None),
        ),
        check_vma=False,
    )
```

```python
import functools

import jax
import jax.numpy as jnp
from jax import lax
from jax.experimental import pallas as pl
from jax.experimental.pallas import tpu as pltpu
from jax.sharding import PartitionSpec as P

MESH = pl.DeviceIdType.MESH
F32 = jnp.float32
BF16 = jnp.bfloat16
MOST = 2
EPS = 1e-05

A = 96

ORDER = (
    (1, 2, 0), (1, 2, 1), (0, 2, 0), (1, 1, 0), (0, 3, 1), (1, 3, 0), (0, 1, 1), (1, 1, 1),
    (0, 3, 0), (1, 3, 1), (0, 1, 0), (0, 2, 1), (1, 0, 0), (1, 0, 1), (0, 0, 1),
)
SLOTS = 96
STEPS = 4


def kernel(
    acts, saved, cot, w, gain, route,
    next_acts, next_grads, wgrad,
    full, acts_v, saved_v, cot_v, chunks, acc, turned, turned_out, slopes, inverse,
    terms, half_a, side_a, far_a, far_b, half_b, side_b, rows_f, rows_b, perm, targets, targets_next, targets_flip,
    send_sem, recv_sem, local_sem,
):
    shard, width = w.shape
    tokens = acts.shape[0]
    chip = 2 * shard
    s = lax.axis_index("section")
    p = lax.axis_index("peer")
    zh, y, c = p // 8, lax.rem(p // 2, 4), lax.rem(p, 2)
    zo, co = 1 - zh, 1 - c
    yp, ym, y2 = lax.rem(y + 1, 4), lax.rem(y + 3, 4), lax.rem(y + 2, 4)
    x, low = lax.rem(s, 4), (s // 4) * 4
    xp, xm, flipped = low + lax.rem(x + 1, 4), low + lax.rem(x + 3, 4), 4 - low + x

    def peer(zz, yy, cc):
        return (s, zz * 8 + yy * 2 + cc)

    right, left, across, core = peer(zh, yp, c), peer(zh, ym, c), peer(zo, y, c), peer(zh, y, co)

    tags = {}
    sent = {}

    def slot(tag):
        return tags.setdefault(tag, len(tags))

    def send(tag, src, dst, device):
        copy = pltpu.make_async_remote_copy(
            src_ref=src, dst_ref=dst, send_sem=send_sem.at[slot(tag)],
            recv_sem=recv_sem.at[slot(tag)], device_id=device, device_id_type=MESH,
        )
        copy.start()
        sent[tag] = copy

    def finished(*names):
        for tag in names:
            copy = sent.pop(tag)
            copy.wait_send()

    def arrive(tag, dst):
        pltpu.make_async_remote_copy(
            src_ref=dst, dst_ref=dst, send_sem=send_sem.at[slot(tag)],
            recv_sem=recv_sem.at[slot(tag)], device_id=core, device_id_type=MESH,
        ).wait_recv()

    loads = [
        pltpu.make_async_copy(src, dst, local_sem.at[i])
        for i, (src, dst) in enumerate(((saved, saved_v), (acts, acts_v), (cot, cot_v)))
    ]
    base = pl.multiple_of(p * shard, 32)
    own_rows = pltpu.make_async_copy(w, full.at[pl.ds(base, shard)], local_sem.at[3])
    own_rows.start()
    for copy in loads:
        copy.start()

    barrier = pltpu.get_barrier_semaphore()
    friends = [peer(zh ^ dz, lax.rem(y + dy, 4), c ^ dc) for dz, dy, dc in ORDER] + [(xp, p), (xm, p)]
    friends += [(flipped, i) for i in range(16)]
    for device in friends:
        pl.semaphore_signal(barrier, inc=1, device_id=device, device_id_type=MESH)
    pl.semaphore_wait(barrier, len(friends))

    def region(zz, yy, cc, lo, hi):
        start = pl.multiple_of((zz * 8 + yy * 2 + cc) * shard + lo, 16)
        return full.at[pl.ds(start, hi - lo)]

    H, M = A // 2, A + (shard - A) // 2
    pieces = {
        "own": (zh, y, 0, shard),
        "zA": (zo, y, 0, A), "yA+": (zh, ym, 0, A), "yA-": (zh, yp, 0, A),
        "yB+": (zh, ym, A, shard), "yB-": (zh, yp, A, shard), "zB": (zo, y, A, shard),
        "A0": (zh, y2, 0, H), "A1": (zh, y2, H, A), "B0": (zh, y2, A, M), "B1": (zh, y2, M, shard),
        "wA+": (zo, ym, 0, A), "wA-": (zo, yp, 0, A), "wA0": (zo, y2, 0, H), "wA1": (zo, y2, H, A),
        "zB+": (zo, ym, A, shard), "zB-": (zo, yp, A, shard),
        "zB0": (zo, y2, A, M), "zB1": (zo, y2, M, shard),
    }

    def give(tag, lo, hi, device):
        send(tag, w.at[pl.ds(lo, hi - lo)], region(zh, y, c, lo, hi), device)

    give("yA+", 0, A, right)
    give("zA", 0, A, across)
    give("yA-", 0, A, left)
    give("yB+", A, shard, right)
    give("zB", A, shard, across)
    give("yB-", A, shard, left)
    give("c:own", 0, shard, core)

    def pass_on(tag, *onward):
        zz, yy, lo, hi = pieces[tag]
        arrive(tag, region(zz, yy, c, lo, hi))
        for new, device in onward:
            _, _, nlo, nhi = pieces[new] if new in ("A0", "A1", "B0", "B1", "wA0", "wA1") else pieces[tag]
            part = region(zz, yy, c, nlo, nhi)
            send(new, part, part, device)
        part = region(zz, yy, c, lo, hi)
        send("c:" + tag, part, part, core)

    def from_core(*names):
        for tag in names:
            zz, yy, lo, hi = pieces[tag]
            arrive("c:" + tag, region(zz, yy, co, lo, hi))

    named = [route[b] for b in range(route.shape[0])]
    block = tokens // len(named)
    lane = lax.broadcasted_iota(jnp.int32, targets.shape, 1)
    spot = jnp.zeros(targets.shape, jnp.int32)
    for b, r in enumerate(named):
        rank = jnp.int32(0)
        for other in named[:b]:
            rank = rank + jnp.where(other == r, 1, 0).astype(jnp.int32)
        first = (r * MOST + rank) * block - b * block
        spot = jnp.where((lane >= b * block) & (lane < (b + 1) * block), lane + first, spot)
    targets[...] = spot
    send("targets", targets, targets_next, (xm, p))
    send("flip", targets, targets_flip, (flipped, p))

    gain_row = gain[...]
    step_rows = 32

    def normalise(source, offset, keep):
        def body(i, carry):
            at = pl.ds(pl.multiple_of(i * step_rows, step_rows), step_rows)
            wide = source[at, :].astype(F32)
            inv = lax.rsqrt(jnp.mean(wide * wide, axis=-1, keepdims=True) + EPS)
            normed = (wide * inv * gain_row).astype(BF16)
            to = pl.ds(pl.multiple_of(offset + i * step_rows, step_rows), step_rows)
            for k in range(width // chip):
                chunks[k, to, :] = normed[:, k * chip:(k + 1) * chip]
            if keep:
                inverse[at, :] = jnp.broadcast_to(inv, (step_rows, inverse.shape[1]))
            return carry

        lax.fori_loop(0, tokens // step_rows, body, 0)

    loads[0].wait()
    normalise(saved_v, 0, True)
    loads[1].wait()
    normalise(acts_v, tokens, False)

    columns = 512

    def multiply(zz, yy, start=False, part_rows=slice(None)):
        k = zz * 4 + yy
        at = pl.ds(pl.multiple_of(k * chip, 64), chip)

        def body(i, carry):
            cols = pl.ds(pl.multiple_of(i * columns, columns), columns)
            part = jnp.dot(chunks[k, part_rows, :], full[at, cols], preferred_element_type=F32)
            acc[part_rows, cols] = part if start else acc[part_rows, cols] + part
            return carry

        lax.fori_loop(0, width // columns, body, 0)

    own_rows.wait()
    from_core("own")
    multiply(zh, y, True)

    pass_on("zA", ("wA+", right), ("wA-", left))
    pass_on("yA+", ("A0", right))
    pass_on("yA-", ("A1", left))

    def turn(k, carry):
        flat = jnp.transpose(chunks[k, 0:tokens, :].astype(F32)).astype(BF16)
        low, high = flat[:shard], flat[shard:]
        to = pl.ds(pl.multiple_of((lax.rem(k, 4) * 2 + k // 4) * shard, 32), shard)
        turned[to, 0:tokens] = jnp.where(c == 0, low, high)
        turned_out[to, :] = jnp.where(c == 0, high, low)
        return carry

    lax.fori_loop(0, width // chip, turn, 0)
    send("turned", turned_out, turned.at[:, pl.ds(tokens, tokens)], core)

    pass_on("yB+", ("B0", right), ("zB+", across))
    pass_on("yB-", ("B1", left), ("zB-", across))
    pass_on("zB")
    from_core("yA+", "yB+")
    multiply(zh, ym)
    pass_on("A0")
    pass_on("A1")
    from_core("yA-", "yB-")
    multiply(zh, yp)
    pass_on("B0", ("zB0", across))
    pass_on("B1", ("zB1", across))
    from_core("zA", "zB")
    multiply(zo, y)
    pass_on("wA+", ("wA0", right))
    pass_on("wA-", ("wA1", left))
    from_core("A0", "A1", "B0", "B1")
    multiply(zh, y2)
    pass_on("zB+")
    pass_on("zB-")
    from_core("wA+", "zB+")
    multiply(zo, ym)
    pass_on("zB0")
    pass_on("zB1")
    from_core("wA-", "zB-")
    multiply(zo, yp)
    pass_on("wA0")
    pass_on("wA1")
    from_core("wA0", "wA1", "zB0", "zB1")
    multiply(zo, y2, part_rows=slice(0, tokens))

    loads[2].wait()
    gathered = list(sent)

    def slope_body(i, carry):
        at = pl.ds(pl.multiple_of(i * step_rows, step_rows), step_rows)
        v = acc[at, :]
        sigma = jax.nn.sigmoid(v)
        slopes[at, :] = (cot_v[at, :].astype(F32) * (sigma * (1.0 + v * (1.0 - sigma)))).astype(BF16)
        return carry

    third = tokens // 3
    for i in range(3):
        lax.fori_loop(i * third // step_rows, (i + 1) * third // step_rows, slope_body, 0)
        send("slope%d" % i, slopes.at[pl.ds(i * third, third)], slopes.at[pl.ds(tokens + i * third, third)], core)

    multiply(zo, y2, part_rows=slice(tokens, None))

    def output_body(i, carry):
        at = pl.ds(pl.multiple_of(i * step_rows, step_rows), step_rows)
        v = acc[pl.ds(pl.multiple_of(tokens + i * step_rows, step_rows), step_rows), :]
        acts_v[at, :] = (acts_v[at, :].astype(F32) + v * jax.nn.sigmoid(v)).astype(BF16)
        return carry

    lax.fori_loop(0, tokens // step_rows, output_body, 0)
    send("forward", acts_v, rows_f, (xp, p))

    arrive("turned", turned.at[:, pl.ds(tokens, tokens)])
    for i in range(3):
        arrive("slope%d" % i, slopes.at[pl.ds(tokens + i * third, third)])

    def term(k, yy):
        at = pl.ds(pl.multiple_of(yy * chip, 64), chip)

        def body(i, carry):
            cols = pl.ds(pl.multiple_of(i * columns, columns), columns)
            part = jnp.dot(turned[at, :], slopes[:, cols], preferred_element_type=F32) / tokens
            part = part.astype(BF16)
            terms[k, 0, :, cols] = part[:shard]
            terms[k, 1, :, cols] = part[shard:]
            return carry

        lax.fori_loop(0, width // columns, body, 0)

    def cross(k):
        send("tB%d" % k, terms.at[k, zo, pl.ds(A, shard - A)], far_b.at[k], across)

    lower, upper = pl.ds(0, H), pl.ds(H, H)
    last, last_low, last_high = pl.ds(A, shard - A), pl.ds(A, M - A), pl.ds(M, shard - M)
    term(0, y2)
    send("tA0", terms.at[0, :, lower], half_a.at[0], right)
    send("tA1", terms.at[0, :, upper], half_a.at[1], left)
    cross(0)
    term(1, yp)
    cross(1)
    term(2, ym)
    cross(2)
    term(3, y)
    cross(3)

    tile = 256

    def back_body(i, carry):
        at = pl.ds(pl.multiple_of(i * tile, tile), tile)
        acc[0:tokens, at] = lax.dot_general(
            slopes[0:tokens, :], full[at, :], (((1,), (1,)), ((), ())), preferred_element_type=F32
        )
        return carry

    lax.fori_loop(0, width // tile, back_body, 0)

    def grad_body(i, carry):
        at = pl.ds(pl.multiple_of(i * step_rows, step_rows), step_rows)
        scaled = acc[at, :] * gain_row
        inv = inverse[at, 0:1]
        unit = saved_v[at, :].astype(F32) * inv
        centre = jnp.mean(scaled * unit, axis=-1, keepdims=True)
        cot_v[at, :] = (cot_v[at, :].astype(F32) + inv * (scaled - unit * centre)).astype(BF16)
        return carry

    lax.fori_loop(0, tokens // step_rows, grad_body, 0)
    send("backward", cot_v, rows_b, (xm, p))

    def add(target, lo, count, extra):
        size = 16

        def body(i, carry):
            at = pl.ds(pl.multiple_of(lo + i * size, size), size)
            here = pl.ds(pl.multiple_of(i * size, size), size)
            target[at, :] = (target[at, :].astype(F32) + extra[here, :].astype(F32)).astype(BF16)
            return carry

        lax.fori_loop(0, count // size, body, 0)

    arrive("tB0", far_b.at[0])
    add(terms.at[0, zh], A, shard - A, far_b.at[0])
    send("tb0", terms.at[0, zh, last_low], half_b.at[0], right)
    send("tb1", terms.at[0, zh, last_high], half_b.at[1], left)
    arrive("tA0", half_a.at[0])
    for z in range(2):
        add(terms.at[1, z], 0, H, half_a.at[0, z])
    send("tA+", terms.at[1, :, pl.ds(0, A)], side_a.at[0], right)
    arrive("tA1", half_a.at[1])
    for z in range(2):
        add(terms.at[2, z], H, H, half_a.at[1, z])
    send("tA-", terms.at[2, :, pl.ds(0, A)], side_a.at[1], left)

    for k, tag, lo, count, device in ((1, "tb0", A, M - A, right), (2, "tb1", M, shard - M, left)):
        arrive("tB%d" % k, far_b.at[k])
        add(terms.at[k, zh], A, shard - A, far_b.at[k])
        arrive(tag, half_b.at[k - 1])
        add(terms.at[k, zh], lo, count, half_b.at[k - 1])
        send("tB" + "?+-"[k], terms.at[k, zh, last], side_b.at[k - 1], device)

    def pack(rows, where, at_row):
        size = 96

        def build(i, carry):
            at = pl.ds(pl.multiple_of(i * size, size), size)
            row = lax.broadcasted_iota(jnp.int32, (size, tokens), 0) + i * size
            perm[at, :] = jnp.where(row == where, 1.0, 0.0).astype(BF16)
            return carry

        lax.fori_loop(0, perm.shape[0] // size, build, 0)

        def body(i, carry):
            cols = pl.ds(pl.multiple_of(i * columns, columns), columns)
            full[at_row:at_row + perm.shape[0], cols] = jnp.dot(
                perm[...], rows[:, cols], preferred_element_type=F32
            ).astype(BF16)
            return carry

        lax.fori_loop(0, width // columns, body, 0)

    share = MOST * block

    def place(ref, number, offset=0):
        return ref.at[pl.ds(pl.multiple_of(offset + number * share, 16), share)]

    def scatter(name, out, offset, sem, flip):
        section = jnp.where(flip, flipped, s)
        for i, (dz, dy, dc) in enumerate(ORDER):
            to = peer(zh ^ dz, lax.rem(y + dy, 4), c ^ dc)[1]
            send("%s%d" % (name, i), place(full, to, offset), place(out, p), (section, to))
        away = pltpu.make_async_remote_copy(
            src_ref=place(full, p, offset), dst_ref=place(out, p), send_sem=send_sem.at[slot(name)],
            recv_sem=recv_sem.at[slot(name)], device_id=(flipped, p), device_id_type=MESH,
        )
        stay = pltpu.make_async_copy(place(full, p, offset), place(out, p), local_sem.at[sem])

        @pl.when(flip)
        def _():
            away.start()

        @pl.when(jnp.logical_not(flip))
        def _():
            stay.start()

        return away, stay, flip

    def collect(name, out, own):
        for i, (dz, dy, dc) in enumerate(ORDER):
            origin = peer(zh ^ dz, lax.rem(y + 4 - dy, 4), c ^ dc)[1]
            arrive("%s%d" % (name, i), place(out, origin))
        away, stay, flip = own

        @pl.when(flip)
        def _():
            away.wait()

        @pl.when(jnp.logical_not(flip))
        def _():
            stay.wait()

    finished(*gathered)

    arrive("tA+", side_a.at[0])
    arrive("tA-", side_a.at[1])
    for z in range(2):
        add(terms.at[3, z], 0, A, side_a.at[0, z])
        add(terms.at[3, z], 0, A, side_a.at[1, z])
    send("tzA", terms.at[3, zo, pl.ds(0, A)], far_a, across)

    arrive("flip", targets_flip)
    arrive("forward", rows_f)
    pack(rows_f, jnp.where(x == 0, targets_flip[0:1, :], targets[0:1, :]), 0)
    finished("backward")
    own_f = scatter("f", next_acts, 0, 4, x == 0)
    arrive("targets", targets_next)
    arrive("backward", rows_b)
    pack(rows_b, targets_next[0:1, :], perm.shape[0])
    finished(*["f%d" % i for i in range(len(ORDER))])
    own_b = scatter("b", next_grads, perm.shape[0], 5, x == 3)

    arrive("tzA", far_a)
    arrive("tB3", far_b.at[3])
    arrive("tB+", side_b.at[0])
    arrive("tB-", side_b.at[1])
    size = 16

    def last_a(i, carry):
        at = pl.ds(pl.multiple_of(i * size, size), size)
        to = pl.ds(pl.multiple_of(tokens + i * size, size), size)
        acc[to, :] = terms[3, zh, at, :].astype(F32) + far_a[at, :].astype(F32)
        return carry

    lax.fori_loop(0, A // size, last_a, 0)

    def last_b(i, carry):
        here = pl.ds(pl.multiple_of(i * size, size), size)
        at = pl.ds(pl.multiple_of(A + i * size, size), size)
        to = pl.ds(pl.multiple_of(tokens + A + i * size, size), size)
        acc[to, :] = (
            (terms[3, zh, at, :].astype(F32) + far_b[3, here, :].astype(F32))
            + (side_b[0, here, :].astype(F32) + side_b[1, here, :].astype(F32))
        )
        return carry

    lax.fori_loop(0, (shard - A) // size, last_b, 0)
    store = pltpu.make_async_copy(acc.at[pl.ds(tokens, shard)], wgrad, local_sem.at[6])
    store.start()

    collect("f", next_acts, own_f)
    collect("b", next_grads, own_b)
    store.wait()
    finished(*list(sent))
    assert len(tags) <= SLOTS, len(tags)


def move(acts, grads, sums, next_acts, next_grads, wgrad):
    next_acts[...] = acts[...]
    next_grads[...] = grads[...]
    wgrad[...] = sums[...]


def local(acts, saved, cotangent, weight, gain, route):
    tokens, width = acts.shape[2:]
    shard = weight.shape[1]
    peers = width // shard
    packed = MOST * tokens
    hbm = pl.BlockSpec(memory_space=pl.ANY)
    v = pltpu.VMEM
    next_acts, next_grads, weight_grad = pl.pallas_call(
        kernel,
        out_shape=(
            jax.ShapeDtypeStruct((packed, width), BF16),
            jax.ShapeDtypeStruct((packed, width), BF16),
            jax.ShapeDtypeStruct((shard, width), F32),
        ),
        in_specs=[hbm] * 4 + [pl.BlockSpec(memory_space=v), pl.BlockSpec(memory_space=pltpu.SMEM)],
        out_specs=(hbm, hbm, hbm),
        scratch_shapes=[
            v((width, width), BF16),
            v((tokens, width), BF16), v((tokens, width), BF16), v((tokens, width), BF16),
            v((peers // 2, 2 * tokens, 2 * shard), BF16),
            v((2 * tokens, width), F32),
            v((width // 2, 2 * tokens), BF16), v((width // 2, tokens), BF16),
            v((2 * tokens, width), BF16),
            v((tokens, 128), F32),
            v((4, 2, shard, width), BF16),
            v((2, 2, A // 2, width), BF16),
            v((2, 2, A, width), BF16),
            v((A, width), BF16),
            v((4, shard - A, width), BF16),
            v((2, (shard - A) // 2, width), BF16),
            v((2, shard - A, width), BF16),
            v((tokens, width), BF16), v((tokens, width), BF16),
            v((packed, tokens), BF16),
            v((8, tokens), jnp.int32), v((8, tokens), jnp.int32), v((8, tokens), jnp.int32),
            pltpu.SemaphoreType.DMA((SLOTS,)),
            pltpu.SemaphoreType.DMA((SLOTS,)),
            pltpu.SemaphoreType.DMA((8,)),
        ],
        compiler_params=pltpu.CompilerParams(
            collective_id=0, has_side_effects=True, vmem_limit_bytes=62 << 20
        ),
        name="tick",
    )(acts[0, 0], saved[0, 0], cotangent[0, 0], weight[0], gain, route[0, 0, :, 0])
    moved = (next_acts, next_grads, weight_grad)
    specs = [pl.BlockSpec((v.shape[0] // STEPS, width), lambda i: (i, 0)) for v in moved]
    next_acts, next_grads, weight_grad = pl.pallas_call(
        move,
        out_shape=tuple(jax.ShapeDtypeStruct(v.shape, v.dtype) for v in moved),
        grid=(STEPS,),
        in_specs=specs,
        out_specs=tuple(specs),
        compiler_params=pltpu.CompilerParams(vmem_limit_bytes=62 << 20),
        name="move",
    )(*moved)
    return (next_acts[None, None], next_grads[None, None], weight_grad[None])


def solution(mesh):
    placed = (
        P("section", "peer", None, None),
        P("section", "peer", None, None),
        P("section", "peer", None, None),
        P("section", "peer", None),
        P("section", None),
        P("section", "peer", None, None),
    )
    return jax.shard_map(
        local,
        mesh=mesh,
        in_specs=placed,
        out_specs=(
            P("section", "peer", None, None),
            P("section", "peer", None, None),
            P("section", "peer", None),
        ),
        check_vma=False,
    )
```

```python
import functools

import jax
import jax.numpy as jnp
from jax import lax
from jax.experimental import pallas as pl
from jax.experimental.pallas import tpu as pltpu
from jax.sharding import PartitionSpec as P

MESH = pl.DeviceIdType.MESH
F32 = jnp.float32
BF16 = jnp.bfloat16
MOST = 2
EPS = 1e-05

A = 96

ORDER = (
    (1, 2, 0), (1, 2, 1), (0, 2, 0), (1, 1, 0), (0, 3, 1), (1, 3, 0), (0, 1, 1), (1, 1, 1),
    (0, 3, 0), (1, 3, 1), (0, 1, 0), (0, 2, 1), (1, 0, 0), (1, 0, 1), (0, 0, 1),
)
SLOTS = 104
STEPS = 4


def kernel(
    acts, saved, cot, w, gain, route,
    next_acts, next_grads, wgrad,
    full, acts_v, saved_v, cot_v, chunks, acc, turned, turned_out, slopes, inverse,
    terms, half_a, side_a, far_a, far_b, half_b, side_b, rows_f, rows_b, perm, targets, targets_next, targets_flip,
    send_sem, recv_sem, local_sem,
):
    shard, width = w.shape
    tokens = acts.shape[0]
    chip = 2 * shard
    s = lax.axis_index("section")
    p = lax.axis_index("peer")
    zh, y, c = p // 8, lax.rem(p // 2, 4), lax.rem(p, 2)
    zo, co = 1 - zh, 1 - c
    yp, ym, y2 = lax.rem(y + 1, 4), lax.rem(y + 3, 4), lax.rem(y + 2, 4)
    x, low = lax.rem(s, 4), (s // 4) * 4
    xp, xm, flipped = low + lax.rem(x + 1, 4), low + lax.rem(x + 3, 4), 4 - low + x

    def peer(zz, yy, cc):
        return (s, zz * 8 + yy * 2 + cc)

    right, left, across, core = peer(zh, yp, c), peer(zh, ym, c), peer(zo, y, c), peer(zh, y, co)

    tags = {}
    sent = {}

    def slot(tag):
        return tags.setdefault(tag, len(tags))

    def send(tag, src, dst, device):
        copy = pltpu.make_async_remote_copy(
            src_ref=src, dst_ref=dst, send_sem=send_sem.at[slot(tag)],
            recv_sem=recv_sem.at[slot(tag)], device_id=device, device_id_type=MESH,
        )
        copy.start()
        sent[tag] = copy

    def finished(*names):
        for tag in names:
            copy = sent.pop(tag)
            copy.wait_send()

    def arrive(tag, dst):
        pltpu.make_async_remote_copy(
            src_ref=dst, dst_ref=dst, send_sem=send_sem.at[slot(tag)],
            recv_sem=recv_sem.at[slot(tag)], device_id=core, device_id_type=MESH,
        ).wait_recv()

    loads = [
        pltpu.make_async_copy(src, dst, local_sem.at[i])
        for i, (src, dst) in enumerate(((saved, saved_v), (acts, acts_v), (cot, cot_v)))
    ]
    base = pl.multiple_of(p * shard, 32)
    own_rows = pltpu.make_async_copy(w, full.at[pl.ds(base, shard)], local_sem.at[3])
    own_rows.start()
    for copy in loads:
        copy.start()

    barrier = pltpu.get_barrier_semaphore()
    friends = [peer(zh ^ dz, lax.rem(y + dy, 4), c ^ dc) for dz, dy, dc in ORDER] + [(xp, p), (xm, p)]
    friends += [(flipped, i) for i in range(16)]
    for device in friends:
        pl.semaphore_signal(barrier, inc=1, device_id=device, device_id_type=MESH)
    pl.semaphore_wait(barrier, len(friends))

    def region(zz, yy, cc, lo, hi):
        start = pl.multiple_of((zz * 8 + yy * 2 + cc) * shard + lo, 16)
        return full.at[pl.ds(start, hi - lo)]

    H, M = A // 2, A + (shard - A) // 2
    pieces = {
        "own": (zh, y, 0, shard),
        "zA": (zo, y, 0, A), "yA+": (zh, ym, 0, A), "yA-": (zh, yp, 0, A),
        "yB+": (zh, ym, A, shard), "yB-": (zh, yp, A, shard), "zB": (zo, y, A, shard),
        "A0": (zh, y2, 0, H), "A1": (zh, y2, H, A), "B0": (zh, y2, A, M), "B1": (zh, y2, M, shard),
        "wA+": (zo, ym, 0, A), "wA-": (zo, yp, 0, A), "wA0": (zo, y2, 0, H), "wA1": (zo, y2, H, A),
        "zB+": (zo, ym, A, shard), "zB-": (zo, yp, A, shard),
        "zB0": (zo, y2, A, M), "zB1": (zo, y2, M, shard),
    }

    def give(tag, lo, hi, device):
        send(tag, w.at[pl.ds(lo, hi - lo)], region(zh, y, c, lo, hi), device)

    give("yA+", 0, A, right)
    give("zA", 0, A, across)
    give("yA-", 0, A, left)
    give("yB+", A, shard, right)
    give("zB", A, shard, across)
    give("yB-", A, shard, left)
    give("c:own", 0, shard, core)

    def pass_on(tag, *onward):
        zz, yy, lo, hi = pieces[tag]
        arrive(tag, region(zz, yy, c, lo, hi))
        for new, device in onward:
            _, _, nlo, nhi = pieces[new] if new in ("A0", "A1", "B0", "B1", "wA0", "wA1") else pieces[tag]
            part = region(zz, yy, c, nlo, nhi)
            send(new, part, part, device)
        part = region(zz, yy, c, lo, hi)
        send("c:" + tag, part, part, core)

    def from_core(*names):
        for tag in names:
            zz, yy, lo, hi = pieces[tag]
            arrive("c:" + tag, region(zz, yy, co, lo, hi))

    named = [route[b] for b in range(route.shape[0])]
    block = tokens // len(named)
    lane = lax.broadcasted_iota(jnp.int32, targets.shape, 1)
    spot = jnp.zeros(targets.shape, jnp.int32)
    for b, r in enumerate(named):
        rank = jnp.int32(0)
        for other in named[:b]:
            rank = rank + jnp.where(other == r, 1, 0).astype(jnp.int32)
        first = (r * MOST + rank) * block - b * block
        spot = jnp.where((lane >= b * block) & (lane < (b + 1) * block), lane + first, spot)
    targets[...] = spot
    send("targets", targets, targets_next, (xm, p))
    send("flip", targets, targets_flip, (flipped, p))

    gain_row = gain[...]
    step_rows = 32

    def normalise(source, offset, keep):
        def body(i, carry):
            at = pl.ds(pl.multiple_of(i * step_rows, step_rows), step_rows)
            wide = source[at, :].astype(F32)
            inv = lax.rsqrt(jnp.mean(wide * wide, axis=-1, keepdims=True) + EPS)
            normed = (wide * inv * gain_row).astype(BF16)
            to = pl.ds(pl.multiple_of(offset + i * step_rows, step_rows), step_rows)
            for k in range(width // chip):
                chunks[k, to, :] = normed[:, k * chip:(k + 1) * chip]
            if keep:
                inverse[at, :] = jnp.broadcast_to(inv, (step_rows, inverse.shape[1]))
            return carry

        lax.fori_loop(0, tokens // step_rows, body, 0)

    loads[0].wait()
    normalise(saved_v, 0, True)
    loads[1].wait()
    normalise(acts_v, tokens, False)

    columns = 512

    def multiply(zz, yy, start=False, part_rows=slice(None)):
        k = zz * 4 + yy
        at = pl.ds(pl.multiple_of(k * chip, 64), chip)

        def body(i, carry):
            cols = pl.ds(pl.multiple_of(i * columns, columns), columns)
            part = jnp.dot(chunks[k, part_rows, :], full[at, cols], preferred_element_type=F32)
            acc[part_rows, cols] = part if start else acc[part_rows, cols] + part
            return carry

        lax.fori_loop(0, width // columns, body, 0)

    own_rows.wait()
    from_core("own")
    multiply(zh, y, True)

    pass_on("zA", ("wA+", right), ("wA-", left))
    pass_on("yA+", ("A0", right))
    pass_on("yA-", ("A1", left))

    def turn(k, carry):
        flat = jnp.transpose(chunks[k, 0:tokens, :].astype(F32)).astype(BF16)
        low, high = flat[:shard], flat[shard:]
        to = pl.ds(pl.multiple_of((lax.rem(k, 4) * 2 + k // 4) * shard, 32), shard)
        turned[to, 0:tokens] = jnp.where(c == 0, low, high)
        turned_out[to, :] = jnp.where(c == 0, high, low)
        return carry

    lax.fori_loop(0, width // chip, turn, 0)
    send("turned", turned_out, turned.at[:, pl.ds(tokens, tokens)], core)

    pass_on("yB+", ("B0", right), ("zB+", across))
    pass_on("yB-", ("B1", left), ("zB-", across))
    pass_on("zB")
    from_core("yA+", "yB+")
    multiply(zh, ym)
    pass_on("A0")
    pass_on("A1")
    from_core("yA-", "yB-")
    multiply(zh, yp)
    pass_on("B0", ("zB0", across))
    pass_on("B1", ("zB1", across))
    from_core("zA", "zB")
    multiply(zo, y)
    pass_on("wA+", ("wA0", right))
    pass_on("wA-", ("wA1", left))
    from_core("A0", "A1", "B0", "B1")
    multiply(zh, y2)
    pass_on("zB+")
    pass_on("zB-")
    from_core("wA+", "zB+")
    multiply(zo, ym)
    pass_on("zB0")
    pass_on("zB1")
    from_core("wA-", "zB-")
    multiply(zo, yp)
    pass_on("wA0")
    pass_on("wA1")
    from_core("wA0", "wA1", "zB0", "zB1")
    multiply(zo, y2, part_rows=slice(0, tokens))

    loads[2].wait()
    gathered = list(sent)

    def slope_body(i, carry):
        at = pl.ds(pl.multiple_of(i * step_rows, step_rows), step_rows)
        v = acc[at, :]
        sigma = jax.nn.sigmoid(v)
        slopes[at, :] = (cot_v[at, :].astype(F32) * (sigma * (1.0 + v * (1.0 - sigma)))).astype(BF16)
        return carry

    third = tokens // 3
    for i in range(3):
        lax.fori_loop(i * third // step_rows, (i + 1) * third // step_rows, slope_body, 0)
        send("slope%d" % i, slopes.at[pl.ds(i * third, third)], slopes.at[pl.ds(tokens + i * third, third)], core)

    multiply(zo, y2, part_rows=slice(tokens, None))

    def output_body(i, carry):
        at = pl.ds(pl.multiple_of(i * step_rows, step_rows), step_rows)
        v = acc[pl.ds(pl.multiple_of(tokens + i * step_rows, step_rows), step_rows), :]
        acts_v[at, :] = (acts_v[at, :].astype(F32) + v * jax.nn.sigmoid(v)).astype(BF16)
        return carry

    for i in range(3):
        part = pl.ds(i * third, third)
        lax.fori_loop(i * third // step_rows, (i + 1) * third // step_rows, output_body, 0)
        send("forward%d" % i, acts_v.at[part], rows_f.at[part], (xp, p))

    arrive("turned", turned.at[:, pl.ds(tokens, tokens)])
    for i in range(3):
        arrive("slope%d" % i, slopes.at[pl.ds(tokens + i * third, third)])

    def term(k, yy):
        at = pl.ds(pl.multiple_of(yy * chip, 64), chip)

        def body(i, carry):
            cols = pl.ds(pl.multiple_of(i * columns, columns), columns)
            part = jnp.dot(turned[at, :], slopes[:, cols], preferred_element_type=F32) / tokens
            part = part.astype(BF16)
            terms[k, 0, :, cols] = part[:shard]
            terms[k, 1, :, cols] = part[shard:]
            return carry

        lax.fori_loop(0, width // columns, body, 0)

    def cross(k):
        send("tB%d" % k, terms.at[k, zo, pl.ds(A, shard - A)], far_b.at[k], across)

    lower, upper = pl.ds(0, H), pl.ds(H, H)
    last, last_low, last_high = pl.ds(A, shard - A), pl.ds(A, M - A), pl.ds(M, shard - M)
    term(0, y2)
    send("tA0", terms.at[0, :, lower], half_a.at[0], right)
    send("tA1", terms.at[0, :, upper], half_a.at[1], left)
    cross(0)
    term(1, yp)
    cross(1)
    term(2, ym)
    cross(2)
    term(3, y)
    cross(3)

    tile = 256

    def back_body(i, carry):
        at = pl.ds(pl.multiple_of(i * tile, tile), tile)
        acc[0:tokens, at] = lax.dot_general(
            slopes[0:tokens, :], full[at, :], (((1,), (1,)), ((), ())), preferred_element_type=F32
        )
        return carry

    lax.fori_loop(0, width // tile, back_body, 0)

    def grad_body(i, carry):
        at = pl.ds(pl.multiple_of(i * step_rows, step_rows), step_rows)
        scaled = acc[at, :] * gain_row
        inv = inverse[at, 0:1]
        unit = saved_v[at, :].astype(F32) * inv
        centre = jnp.mean(scaled * unit, axis=-1, keepdims=True)
        cot_v[at, :] = (cot_v[at, :].astype(F32) + inv * (scaled - unit * centre)).astype(BF16)
        return carry

    for i in range(3):
        part = pl.ds(i * third, third)
        lax.fori_loop(i * third // step_rows, (i + 1) * third // step_rows, grad_body, 0)
        send("backward%d" % i, cot_v.at[part], rows_b.at[part], (xm, p))

    def add(target, lo, count, extra):
        size = 16

        def body(i, carry):
            at = pl.ds(pl.multiple_of(lo + i * size, size), size)
            here = pl.ds(pl.multiple_of(i * size, size), size)
            target[at, :] = (target[at, :].astype(F32) + extra[here, :].astype(F32)).astype(BF16)
            return carry

        lax.fori_loop(0, count // size, body, 0)

    arrive("tB0", far_b.at[0])
    add(terms.at[0, zh], A, shard - A, far_b.at[0])
    send("tb0", terms.at[0, zh, last_low], half_b.at[0], right)
    send("tb1", terms.at[0, zh, last_high], half_b.at[1], left)
    arrive("tA0", half_a.at[0])
    for z in range(2):
        add(terms.at[1, z], 0, H, half_a.at[0, z])
    send("tA+", terms.at[1, :, pl.ds(0, A)], side_a.at[0], right)
    arrive("tA1", half_a.at[1])
    for z in range(2):
        add(terms.at[2, z], H, H, half_a.at[1, z])
    send("tA-", terms.at[2, :, pl.ds(0, A)], side_a.at[1], left)

    for k, tag, lo, count, device in ((1, "tb0", A, M - A, right), (2, "tb1", M, shard - M, left)):
        arrive("tB%d" % k, far_b.at[k])
        add(terms.at[k, zh], A, shard - A, far_b.at[k])
        arrive(tag, half_b.at[k - 1])
        add(terms.at[k, zh], lo, count, half_b.at[k - 1])
        send("tB" + "?+-"[k], terms.at[k, zh, last], side_b.at[k - 1], device)

    def pack(rows, where, at_row):
        size = 96

        def build(i, carry):
            at = pl.ds(pl.multiple_of(i * size, size), size)
            row = lax.broadcasted_iota(jnp.int32, (size, tokens), 0) + i * size
            perm[at, :] = jnp.where(row == where, 1.0, 0.0).astype(BF16)
            return carry

        lax.fori_loop(0, perm.shape[0] // size, build, 0)

        def body(i, carry):
            cols = pl.ds(pl.multiple_of(i * columns, columns), columns)
            full[at_row:at_row + perm.shape[0], cols] = jnp.dot(
                perm[...], rows[:, cols], preferred_element_type=F32
            ).astype(BF16)
            return carry

        lax.fori_loop(0, width // columns, body, 0)

    share = MOST * block

    def place(ref, number, offset=0):
        return ref.at[pl.ds(pl.multiple_of(offset + number * share, 16), share)]

    def scatter(name, out, offset, sem, flip):
        section = jnp.where(flip, flipped, s)
        for i, (dz, dy, dc) in enumerate(ORDER):
            to = peer(zh ^ dz, lax.rem(y + dy, 4), c ^ dc)[1]
            send("%s%d" % (name, i), place(full, to, offset), place(out, p), (section, to))
        away = pltpu.make_async_remote_copy(
            src_ref=place(full, p, offset), dst_ref=place(out, p), send_sem=send_sem.at[slot(name)],
            recv_sem=recv_sem.at[slot(name)], device_id=(flipped, p), device_id_type=MESH,
        )
        stay = pltpu.make_async_copy(place(full, p, offset), place(out, p), local_sem.at[sem])

        @pl.when(flip)
        def _():
            away.start()

        @pl.when(jnp.logical_not(flip))
        def _():
            stay.start()

        return away, stay, flip

    def collect(name, out, own):
        for i, (dz, dy, dc) in enumerate(ORDER):
            origin = peer(zh ^ dz, lax.rem(y + 4 - dy, 4), c ^ dc)[1]
            arrive("%s%d" % (name, i), place(out, origin))
        away, stay, flip = own

        @pl.when(flip)
        def _():
            away.wait()

        @pl.when(jnp.logical_not(flip))
        def _():
            stay.wait()

    finished(*gathered)

    arrive("tA+", side_a.at[0])
    arrive("tA-", side_a.at[1])
    for z in range(2):
        add(terms.at[3, z], 0, A, side_a.at[0, z])
        add(terms.at[3, z], 0, A, side_a.at[1, z])
    send("tzA", terms.at[3, zo, pl.ds(0, A)], far_a, across)

    arrive("flip", targets_flip)
    for i in range(3):
        arrive("forward%d" % i, rows_f.at[pl.ds(i * third, third)])
    pack(rows_f, jnp.where(x == 0, targets_flip[0:1, :], targets[0:1, :]), 0)
    finished("backward0", "backward1", "backward2")
    own_f = scatter("f", next_acts, 0, 4, x == 0)
    arrive("targets", targets_next)
    for i in range(3):
        arrive("backward%d" % i, rows_b.at[pl.ds(i * third, third)])
    pack(rows_b, targets_next[0:1, :], perm.shape[0])
    finished(*["f%d" % i for i in range(len(ORDER))])
    own_b = scatter("b", next_grads, perm.shape[0], 5, x == 3)

    arrive("tzA", far_a)
    arrive("tB3", far_b.at[3])
    arrive("tB+", side_b.at[0])
    arrive("tB-", side_b.at[1])
    size = 16

    def last_a(i, carry):
        at = pl.ds(pl.multiple_of(i * size, size), size)
        to = pl.ds(pl.multiple_of(tokens + i * size, size), size)
        acc[to, :] = terms[3, zh, at, :].astype(F32) + far_a[at, :].astype(F32)
        return carry

    lax.fori_loop(0, A // size, last_a, 0)

    def last_b(i, carry):
        here = pl.ds(pl.multiple_of(i * size, size), size)
        at = pl.ds(pl.multiple_of(A + i * size, size), size)
        to = pl.ds(pl.multiple_of(tokens + A + i * size, size), size)
        acc[to, :] = (
            (terms[3, zh, at, :].astype(F32) + far_b[3, here, :].astype(F32))
            + (side_b[0, here, :].astype(F32) + side_b[1, here, :].astype(F32))
        )
        return carry

    lax.fori_loop(0, (shard - A) // size, last_b, 0)
    store = pltpu.make_async_copy(acc.at[pl.ds(tokens, shard)], wgrad, local_sem.at[6])
    store.start()

    collect("f", next_acts, own_f)
    collect("b", next_grads, own_b)
    store.wait()
    finished(*list(sent))
    assert len(tags) <= SLOTS, len(tags)


def move(acts, grads, sums, next_acts, next_grads, wgrad):
    next_acts[...] = acts[...]
    next_grads[...] = grads[...]
    wgrad[...] = sums[...]


def local(acts, saved, cotangent, weight, gain, route):
    tokens, width = acts.shape[2:]
    shard = weight.shape[1]
    peers = width // shard
    packed = MOST * tokens
    hbm = pl.BlockSpec(memory_space=pl.ANY)
    v = pltpu.VMEM
    next_acts, next_grads, weight_grad = pl.pallas_call(
        kernel,
        out_shape=(
            jax.ShapeDtypeStruct((packed, width), BF16),
            jax.ShapeDtypeStruct((packed, width), BF16),
            jax.ShapeDtypeStruct((shard, width), F32),
        ),
        in_specs=[hbm] * 4 + [pl.BlockSpec(memory_space=v), pl.BlockSpec(memory_space=pltpu.SMEM)],
        out_specs=(hbm, hbm, hbm),
        scratch_shapes=[
            v((width, width), BF16),
            v((tokens, width), BF16), v((tokens, width), BF16), v((tokens, width), BF16),
            v((peers // 2, 2 * tokens, 2 * shard), BF16),
            v((2 * tokens, width), F32),
            v((width // 2, 2 * tokens), BF16), v((width // 2, tokens), BF16),
            v((2 * tokens, width), BF16),
            v((tokens, 128), F32),
            v((4, 2, shard, width), BF16),
            v((2, 2, A // 2, width), BF16),
            v((2, 2, A, width), BF16),
            v((A, width), BF16),
            v((4, shard - A, width), BF16),
            v((2, (shard - A) // 2, width), BF16),
            v((2, shard - A, width), BF16),
            v((tokens, width), BF16), v((tokens, width), BF16),
            v((packed, tokens), BF16),
            v((8, tokens), jnp.int32), v((8, tokens), jnp.int32), v((8, tokens), jnp.int32),
            pltpu.SemaphoreType.DMA((SLOTS,)),
            pltpu.SemaphoreType.DMA((SLOTS,)),
            pltpu.SemaphoreType.DMA((8,)),
        ],
        compiler_params=pltpu.CompilerParams(
            collective_id=0, has_side_effects=True, vmem_limit_bytes=62 << 20
        ),
        name="tick",
    )(acts[0, 0], saved[0, 0], cotangent[0, 0], weight[0], gain, route[0, 0, :, 0])
    moved = (next_acts, next_grads, weight_grad)
    specs = [pl.BlockSpec((v.shape[0] // STEPS, width), lambda i: (i, 0)) for v in moved]
    next_acts, next_grads, weight_grad = pl.pallas_call(
        move,
        out_shape=tuple(jax.ShapeDtypeStruct(v.shape, v.dtype) for v in moved),
        grid=(STEPS,),
        in_specs=specs,
        out_specs=tuple(specs),
        compiler_params=pltpu.CompilerParams(vmem_limit_bytes=62 << 20),
        name="move",
    )(*moved)
    return (next_acts[None, None], next_grads[None, None], weight_grad[None])


def solution(mesh):
    placed = (
        P("section", "peer", None, None),
        P("section", "peer", None, None),
        P("section", "peer", None, None),
        P("section", "peer", None),
        P("section", None),
        P("section", "peer", None, None),
    )
    return jax.shard_map(
        local,
        mesh=mesh,
        in_specs=placed,
        out_specs=(
            P("section", "peer", None, None),
            P("section", "peer", None, None),
            P("section", "peer", None),
        ),
        check_vma=False,
    )
```

```python
import functools

import jax
import jax.numpy as jnp
from jax import lax
from jax.experimental import pallas as pl
from jax.experimental.pallas import tpu as pltpu
from jax.sharding import PartitionSpec as P

MESH = pl.DeviceIdType.MESH
F32 = jnp.float32
BF16 = jnp.bfloat16
MOST = 2
EPS = 1e-05

A = 96

ORDER = (
    (1, 2, 0), (1, 2, 1), (0, 2, 0), (1, 1, 0), (0, 3, 1), (1, 3, 0), (0, 1, 1), (1, 1, 1),
    (0, 3, 0), (1, 3, 1), (0, 1, 0), (0, 2, 1), (1, 0, 0), (1, 0, 1), (0, 0, 1),
)
SLOTS = 120
STEPS = 4


def kernel(
    acts, saved, cot, w, gain, route,
    next_acts, next_grads, wgrad,
    full, acts_v, saved_v, cot_v, chunks, acc, turned, turned_out, slopes, inverse,
    terms, half_a, side_a, far_a, far_b, half_b, side_b, rows_f, rows_b, perm, targets, targets_next, targets_flip,
    send_sem, recv_sem, local_sem,
):
    shard, width = w.shape
    tokens = acts.shape[0]
    chip = 2 * shard
    s = lax.axis_index("section")
    p = lax.axis_index("peer")
    zh, y, c = p // 8, lax.rem(p // 2, 4), lax.rem(p, 2)
    zo, co = 1 - zh, 1 - c
    yp, ym, y2 = lax.rem(y + 1, 4), lax.rem(y + 3, 4), lax.rem(y + 2, 4)
    x, low = lax.rem(s, 4), (s // 4) * 4
    xp, xm, flipped = low + lax.rem(x + 1, 4), low + lax.rem(x + 3, 4), 4 - low + x

    def peer(zz, yy, cc):
        return (s, zz * 8 + yy * 2 + cc)

    right, left, across, core = peer(zh, yp, c), peer(zh, ym, c), peer(zo, y, c), peer(zh, y, co)

    tags = {}
    sent = {}

    def slot(tag):
        return tags.setdefault(tag, len(tags))

    def send(tag, src, dst, device):
        copy = pltpu.make_async_remote_copy(
            src_ref=src, dst_ref=dst, send_sem=send_sem.at[slot(tag)],
            recv_sem=recv_sem.at[slot(tag)], device_id=device, device_id_type=MESH,
        )
        copy.start()
        sent[tag] = copy

    def finished(*names):
        for tag in names:
            copy = sent.pop(tag)
            copy.wait_send()

    def arrive(tag, dst):
        pltpu.make_async_remote_copy(
            src_ref=dst, dst_ref=dst, send_sem=send_sem.at[slot(tag)],
            recv_sem=recv_sem.at[slot(tag)], device_id=core, device_id_type=MESH,
        ).wait_recv()

    loads = [
        pltpu.make_async_copy(src, dst, local_sem.at[i])
        for i, (src, dst) in enumerate(((saved, saved_v), (acts, acts_v), (cot, cot_v)))
    ]
    base = pl.multiple_of(p * shard, 32)
    own_rows = pltpu.make_async_copy(w, full.at[pl.ds(base, shard)], local_sem.at[3])
    own_rows.start()
    for copy in loads:
        copy.start()

    barrier = pltpu.get_barrier_semaphore()
    friends = [peer(zh ^ dz, lax.rem(y + dy, 4), c ^ dc) for dz, dy, dc in ORDER] + [(xp, p), (xm, p)]
    friends += [(flipped, i) for i in range(16)]
    for device in friends:
        pl.semaphore_signal(barrier, inc=1, device_id=device, device_id_type=MESH)
    pl.semaphore_wait(barrier, len(friends))

    def region(zz, yy, cc, lo, hi):
        start = pl.multiple_of((zz * 8 + yy * 2 + cc) * shard + lo, 16)
        return full.at[pl.ds(start, hi - lo)]

    H, M = A // 2, A + (shard - A) // 2
    pieces = {
        "own": (zh, y, 0, shard),
        "zA": (zo, y, 0, A), "yA+": (zh, ym, 0, A), "yA-": (zh, yp, 0, A),
        "yB+": (zh, ym, A, shard), "yB-": (zh, yp, A, shard), "zB": (zo, y, A, shard),
        "A0": (zh, y2, 0, H), "A1": (zh, y2, H, A), "B0": (zh, y2, A, M), "B1": (zh, y2, M, shard),
        "wA+": (zo, ym, 0, A), "wA-": (zo, yp, 0, A), "wA0": (zo, y2, 0, H), "wA1": (zo, y2, H, A),
        "zB+": (zo, ym, A, shard), "zB-": (zo, yp, A, shard),
        "zB0": (zo, y2, A, M), "zB1": (zo, y2, M, shard),
    }

    def give(tag, lo, hi, device):
        send(tag, w.at[pl.ds(lo, hi - lo)], region(zh, y, c, lo, hi), device)

    give("yA+", 0, A, right)
    give("zA", 0, A, across)
    give("yA-", 0, A, left)
    give("yB+", A, shard, right)
    give("zB", A, shard, across)
    give("yB-", A, shard, left)
    give("c:own", 0, shard, core)

    def pass_on(tag, *onward):
        zz, yy, lo, hi = pieces[tag]
        arrive(tag, region(zz, yy, c, lo, hi))
        for new, device in onward:
            _, _, nlo, nhi = pieces[new] if new in ("A0", "A1", "B0", "B1", "wA0", "wA1") else pieces[tag]
            part = region(zz, yy, c, nlo, nhi)
            send(new, part, part, device)
        part = region(zz, yy, c, lo, hi)
        send("c:" + tag, part, part, core)

    def from_core(*names):
        for tag in names:
            zz, yy, lo, hi = pieces[tag]
            arrive("c:" + tag, region(zz, yy, co, lo, hi))

    named = [route[b] for b in range(route.shape[0])]
    block = tokens // len(named)
    lane = lax.broadcasted_iota(jnp.int32, targets.shape, 1)
    spot = jnp.zeros(targets.shape, jnp.int32)
    for b, r in enumerate(named):
        rank = jnp.int32(0)
        for other in named[:b]:
            rank = rank + jnp.where(other == r, 1, 0).astype(jnp.int32)
        first = (r * MOST + rank) * block - b * block
        spot = jnp.where((lane >= b * block) & (lane < (b + 1) * block), lane + first, spot)
    targets[...] = spot
    send("targets", targets, targets_next, (xm, p))
    send("flip", targets, targets_flip, (flipped, p))

    gain_row = gain[...]
    step_rows = 32

    def normalise(source, offset, keep):
        def body(i, carry):
            at = pl.ds(pl.multiple_of(i * step_rows, step_rows), step_rows)
            wide = source[at, :].astype(F32)
            inv = lax.rsqrt(jnp.mean(wide * wide, axis=-1, keepdims=True) + EPS)
            normed = (wide * inv * gain_row).astype(BF16)
            to = pl.ds(pl.multiple_of(offset + i * step_rows, step_rows), step_rows)
            for k in range(width // chip):
                chunks[k, to, :] = normed[:, k * chip:(k + 1) * chip]
            if keep:
                inverse[at, :] = jnp.broadcast_to(inv, (step_rows, inverse.shape[1]))
            return carry

        lax.fori_loop(0, tokens // step_rows, body, 0)

    loads[0].wait()
    normalise(saved_v, 0, True)
    loads[1].wait()
    normalise(acts_v, tokens, False)

    columns = 512

    def multiply(zz, yy, start=False, part_rows=slice(None)):
        k = zz * 4 + yy
        at = pl.ds(pl.multiple_of(k * chip, 64), chip)

        def body(i, carry):
            cols = pl.ds(pl.multiple_of(i * columns, columns), columns)
            part = jnp.dot(chunks[k, part_rows, :], full[at, cols], preferred_element_type=F32)
            acc[part_rows, cols] = part if start else acc[part_rows, cols] + part
            return carry

        lax.fori_loop(0, width // columns, body, 0)

    own_rows.wait()
    from_core("own")
    multiply(zh, y, True)

    pass_on("zA", ("wA+", right), ("wA-", left))
    pass_on("yA+", ("A0", right))
    pass_on("yA-", ("A1", left))

    def turn(k, carry):
        flat = jnp.transpose(chunks[k, 0:tokens, :].astype(F32)).astype(BF16)
        low, high = flat[:shard], flat[shard:]
        to = pl.ds(pl.multiple_of((lax.rem(k, 4) * 2 + k // 4) * shard, 32), shard)
        turned[to, 0:tokens] = jnp.where(c == 0, low, high)
        turned_out[to, :] = jnp.where(c == 0, high, low)
        return carry

    lax.fori_loop(0, width // chip, turn, 0)
    send("turned", turned_out, turned.at[:, pl.ds(tokens, tokens)], core)

    pass_on("yB+", ("B0", right), ("zB+", across))
    pass_on("yB-", ("B1", left), ("zB-", across))
    pass_on("zB")
    from_core("yA+", "yB+")
    multiply(zh, ym)
    pass_on("A0")
    pass_on("A1")
    from_core("yA-", "yB-")
    multiply(zh, yp)
    pass_on("B0", ("zB0", across))
    pass_on("B1", ("zB1", across))
    from_core("zA", "zB")
    multiply(zo, y)
    pass_on("wA+", ("wA0", right))
    pass_on("wA-", ("wA1", left))
    from_core("A0", "A1", "B0", "B1")
    multiply(zh, y2)
    pass_on("zB+")
    pass_on("zB-")
    from_core("wA+", "zB+")
    multiply(zo, ym)
    pass_on("zB0")
    pass_on("zB1")
    from_core("wA-", "zB-")
    multiply(zo, yp)
    pass_on("wA0")
    pass_on("wA1")
    from_core("wA0", "wA1", "zB0", "zB1")
    multiply(zo, y2, part_rows=slice(0, tokens))

    loads[2].wait()
    gathered = list(sent)

    def slope_body(i, carry):
        at = pl.ds(pl.multiple_of(i * step_rows, step_rows), step_rows)
        v = acc[at, :]
        sigma = jax.nn.sigmoid(v)
        slopes[at, :] = (cot_v[at, :].astype(F32) * (sigma * (1.0 + v * (1.0 - sigma)))).astype(BF16)
        return carry

    sixth = tokens // 6
    for i in range(6):
        lax.fori_loop(i * sixth // step_rows, (i + 1) * sixth // step_rows, slope_body, 0)
        send("slope%d" % i, slopes.at[pl.ds(i * sixth, sixth)], slopes.at[pl.ds(tokens + i * sixth, sixth)], core)

    multiply(zo, y2, part_rows=slice(tokens, None))

    def output_body(i, carry):
        at = pl.ds(pl.multiple_of(i * step_rows, step_rows), step_rows)
        v = acc[pl.ds(pl.multiple_of(tokens + i * step_rows, step_rows), step_rows), :]
        acts_v[at, :] = (acts_v[at, :].astype(F32) + v * jax.nn.sigmoid(v)).astype(BF16)
        return carry

    for i in range(6):
        part = pl.ds(i * sixth, sixth)
        lax.fori_loop(i * sixth // step_rows, (i + 1) * sixth // step_rows, output_body, 0)
        send("forward%d" % i, acts_v.at[part], rows_f.at[part], (xp, p))

    arrive("turned", turned.at[:, pl.ds(tokens, tokens)])
    for i in range(6):
        arrive("slope%d" % i, slopes.at[pl.ds(tokens + i * sixth, sixth)])

    def term(k, yy):
        at = pl.ds(pl.multiple_of(yy * chip, 64), chip)

        def body(i, carry):
            cols = pl.ds(pl.multiple_of(i * columns, columns), columns)
            part = jnp.dot(turned[at, :], slopes[:, cols], preferred_element_type=F32) / tokens
            part = part.astype(BF16)
            terms[k, 0, :, cols] = part[:shard]
            terms[k, 1, :, cols] = part[shard:]
            return carry

        lax.fori_loop(0, width // columns, body, 0)

    def cross(k):
        send("tB%d" % k, terms.at[k, zo, pl.ds(A, shard - A)], far_b.at[k], across)

    lower, upper = pl.ds(0, H), pl.ds(H, H)
    last, last_low, last_high = pl.ds(A, shard - A), pl.ds(A, M - A), pl.ds(M, shard - M)
    term(0, y2)
    send("tA0", terms.at[0, :, lower], half_a.at[0], right)
    send("tA1", terms.at[0, :, upper], half_a.at[1], left)
    cross(0)
    term(1, yp)
    cross(1)
    term(2, ym)
    cross(2)
    term(3, y)
    cross(3)

    tile = 256

    def back_body(i, carry):
        at = pl.ds(pl.multiple_of(i * tile, tile), tile)
        acc[0:tokens, at] = lax.dot_general(
            slopes[0:tokens, :], full[at, :], (((1,), (1,)), ((), ())), preferred_element_type=F32
        )
        return carry

    lax.fori_loop(0, width // tile, back_body, 0)

    def grad_body(i, carry):
        at = pl.ds(pl.multiple_of(i * step_rows, step_rows), step_rows)
        scaled = acc[at, :] * gain_row
        inv = inverse[at, 0:1]
        unit = saved_v[at, :].astype(F32) * inv
        centre = jnp.mean(scaled * unit, axis=-1, keepdims=True)
        cot_v[at, :] = (cot_v[at, :].astype(F32) + inv * (scaled - unit * centre)).astype(BF16)
        return carry

    for i in range(6):
        part = pl.ds(i * sixth, sixth)
        lax.fori_loop(i * sixth // step_rows, (i + 1) * sixth // step_rows, grad_body, 0)
        send("backward%d" % i, cot_v.at[part], rows_b.at[part], (xm, p))

    def add(target, lo, count, extra):
        size = 16

        def body(i, carry):
            at = pl.ds(pl.multiple_of(lo + i * size, size), size)
            here = pl.ds(pl.multiple_of(i * size, size), size)
            target[at, :] = (target[at, :].astype(F32) + extra[here, :].astype(F32)).astype(BF16)
            return carry

        lax.fori_loop(0, count // size, body, 0)

    arrive("tB0", far_b.at[0])
    add(terms.at[0, zh], A, shard - A, far_b.at[0])
    send("tb0", terms.at[0, zh, last_low], half_b.at[0], right)
    send("tb1", terms.at[0, zh, last_high], half_b.at[1], left)
    arrive("tA0", half_a.at[0])
    for z in range(2):
        add(terms.at[1, z], 0, H, half_a.at[0, z])
    send("tA+", terms.at[1, :, pl.ds(0, A)], side_a.at[0], right)
    arrive("tA1", half_a.at[1])
    for z in range(2):
        add(terms.at[2, z], H, H, half_a.at[1, z])
    send("tA-", terms.at[2, :, pl.ds(0, A)], side_a.at[1], left)

    for k, tag, lo, count, device in ((1, "tb0", A, M - A, right), (2, "tb1", M, shard - M, left)):
        arrive("tB%d" % k, far_b.at[k])
        add(terms.at[k, zh], A, shard - A, far_b.at[k])
        arrive(tag, half_b.at[k - 1])
        add(terms.at[k, zh], lo, count, half_b.at[k - 1])
        send("tB" + "?+-"[k], terms.at[k, zh, last], side_b.at[k - 1], device)

    def pack(rows, where, at_row):
        size = 96

        def build(i, carry):
            at = pl.ds(pl.multiple_of(i * size, size), size)
            row = lax.broadcasted_iota(jnp.int32, (size, tokens), 0) + i * size
            perm[at, :] = jnp.where(row == where, 1.0, 0.0).astype(BF16)
            return carry

        lax.fori_loop(0, perm.shape[0] // size, build, 0)

        def body(i, carry):
            cols = pl.ds(pl.multiple_of(i * columns, columns), columns)
            full[at_row:at_row + perm.shape[0], cols] = jnp.dot(
                perm[...], rows[:, cols], preferred_element_type=F32
            ).astype(BF16)
            return carry

        lax.fori_loop(0, width // columns, body, 0)

    share = MOST * block

    def place(ref, number, offset=0):
        return ref.at[pl.ds(pl.multiple_of(offset + number * share, 16), share)]

    def scatter(name, out, offset, sem, flip):
        section = jnp.where(flip, flipped, s)
        for i, (dz, dy, dc) in enumerate(ORDER):
            to = peer(zh ^ dz, lax.rem(y + dy, 4), c ^ dc)[1]
            send("%s%d" % (name, i), place(full, to, offset), place(out, p), (section, to))
        away = pltpu.make_async_remote_copy(
            src_ref=place(full, p, offset), dst_ref=place(out, p), send_sem=send_sem.at[slot(name)],
            recv_sem=recv_sem.at[slot(name)], device_id=(flipped, p), device_id_type=MESH,
        )
        stay = pltpu.make_async_copy(place(full, p, offset), place(out, p), local_sem.at[sem])

        @pl.when(flip)
        def _():
            away.start()

        @pl.when(jnp.logical_not(flip))
        def _():
            stay.start()

        return away, stay, flip

    def collect(name, out, own):
        for i, (dz, dy, dc) in enumerate(ORDER):
            origin = peer(zh ^ dz, lax.rem(y + 4 - dy, 4), c ^ dc)[1]
            arrive("%s%d" % (name, i), place(out, origin))
        away, stay, flip = own

        @pl.when(flip)
        def _():
            away.wait()

        @pl.when(jnp.logical_not(flip))
        def _():
            stay.wait()

    finished(*gathered)

    arrive("tA+", side_a.at[0])
    arrive("tA-", side_a.at[1])
    for z in range(2):
        add(terms.at[3, z], 0, A, side_a.at[0, z])
        add(terms.at[3, z], 0, A, side_a.at[1, z])
    send("tzA", terms.at[3, zo, pl.ds(0, A)], far_a, across)

    arrive("flip", targets_flip)
    for i in range(6):
        arrive("forward%d" % i, rows_f.at[pl.ds(i * sixth, sixth)])
    pack(rows_f, jnp.where(x == 0, targets_flip[0:1, :], targets[0:1, :]), 0)
    finished(*["backward%d" % i for i in range(6)])
    own_f = scatter("f", next_acts, 0, 4, x == 0)
    arrive("targets", targets_next)
    for i in range(6):
        arrive("backward%d" % i, rows_b.at[pl.ds(i * sixth, sixth)])
    pack(rows_b, targets_next[0:1, :], perm.shape[0])
    finished(*["f%d" % i for i in range(len(ORDER))])
    own_b = scatter("b", next_grads, perm.shape[0], 5, x == 3)

    arrive("tzA", far_a)
    arrive("tB3", far_b.at[3])
    arrive("tB+", side_b.at[0])
    arrive("tB-", side_b.at[1])
    size = 16

    def last_a(i, carry):
        at = pl.ds(pl.multiple_of(i * size, size), size)
        to = pl.ds(pl.multiple_of(tokens + i * size, size), size)
        acc[to, :] = terms[3, zh, at, :].astype(F32) + far_a[at, :].astype(F32)
        return carry

    lax.fori_loop(0, A // size, last_a, 0)

    def last_b(i, carry):
        here = pl.ds(pl.multiple_of(i * size, size), size)
        at = pl.ds(pl.multiple_of(A + i * size, size), size)
        to = pl.ds(pl.multiple_of(tokens + A + i * size, size), size)
        acc[to, :] = (
            (terms[3, zh, at, :].astype(F32) + far_b[3, here, :].astype(F32))
            + (side_b[0, here, :].astype(F32) + side_b[1, here, :].astype(F32))
        )
        return carry

    lax.fori_loop(0, (shard - A) // size, last_b, 0)
    store = pltpu.make_async_copy(acc.at[pl.ds(tokens, shard)], wgrad, local_sem.at[6])
    store.start()

    collect("f", next_acts, own_f)
    collect("b", next_grads, own_b)
    store.wait()
    finished(*list(sent))
    assert len(tags) <= SLOTS, len(tags)


def move(acts, grads, sums, next_acts, next_grads, wgrad):
    next_acts[...] = acts[...]
    next_grads[...] = grads[...]
    wgrad[...] = sums[...]


def local(acts, saved, cotangent, weight, gain, route):
    tokens, width = acts.shape[2:]
    shard = weight.shape[1]
    peers = width // shard
    packed = MOST * tokens
    hbm = pl.BlockSpec(memory_space=pl.ANY)
    v = pltpu.VMEM
    next_acts, next_grads, weight_grad = pl.pallas_call(
        kernel,
        out_shape=(
            jax.ShapeDtypeStruct((packed, width), BF16),
            jax.ShapeDtypeStruct((packed, width), BF16),
            jax.ShapeDtypeStruct((shard, width), F32),
        ),
        in_specs=[hbm] * 4 + [pl.BlockSpec(memory_space=v), pl.BlockSpec(memory_space=pltpu.SMEM)],
        out_specs=(hbm, hbm, hbm),
        scratch_shapes=[
            v((width, width), BF16),
            v((tokens, width), BF16), v((tokens, width), BF16), v((tokens, width), BF16),
            v((peers // 2, 2 * tokens, 2 * shard), BF16),
            v((2 * tokens, width), F32),
            v((width // 2, 2 * tokens), BF16), v((width // 2, tokens), BF16),
            v((2 * tokens, width), BF16),
            v((tokens, 128), F32),
            v((4, 2, shard, width), BF16),
            v((2, 2, A // 2, width), BF16),
            v((2, 2, A, width), BF16),
            v((A, width), BF16),
            v((4, shard - A, width), BF16),
            v((2, (shard - A) // 2, width), BF16),
            v((2, shard - A, width), BF16),
            v((tokens, width), BF16), v((tokens, width), BF16),
            v((packed, tokens), BF16),
            v((8, tokens), jnp.int32), v((8, tokens), jnp.int32), v((8, tokens), jnp.int32),
            pltpu.SemaphoreType.DMA((SLOTS,)),
            pltpu.SemaphoreType.DMA((SLOTS,)),
            pltpu.SemaphoreType.DMA((8,)),
        ],
        compiler_params=pltpu.CompilerParams(
            collective_id=0, has_side_effects=True, vmem_limit_bytes=62 << 20
        ),
        name="tick",
    )(acts[0, 0], saved[0, 0], cotangent[0, 0], weight[0], gain, route[0, 0, :, 0])
    moved = (next_acts, next_grads, weight_grad)
    specs = [pl.BlockSpec((v.shape[0] // STEPS, width), lambda i: (i, 0)) for v in moved]
    next_acts, next_grads, weight_grad = pl.pallas_call(
        move,
        out_shape=tuple(jax.ShapeDtypeStruct(v.shape, v.dtype) for v in moved),
        grid=(STEPS,),
        in_specs=specs,
        out_specs=tuple(specs),
        compiler_params=pltpu.CompilerParams(vmem_limit_bytes=62 << 20),
        name="move",
    )(*moved)
    return (next_acts[None, None], next_grads[None, None], weight_grad[None])


def solution(mesh):
    placed = (
        P("section", "peer", None, None),
        P("section", "peer", None, None),
        P("section", "peer", None, None),
        P("section", "peer", None),
        P("section", None),
        P("section", "peer", None, None),
    )
    return jax.shard_map(
        local,
        mesh=mesh,
        in_specs=placed,
        out_specs=(
            P("section", "peer", None, None),
            P("section", "peer", None, None),
            P("section", "peer", None),
        ),
        check_vma=False,
    )
```
